128 devices in a mesh: fsdp: 32 (over x, y_lo, z), tp: 4 (over y_hi, core).
Axes of the slice: x: 4, y: 4 (y_hi: 2, y_lo: 2; y = y_hi * 2 + y_lo), z: 4, core: 2. Of those that a mesh axis runs over, the one named last changes fastest.
Arguments:
- tokens: bfloat16 [16384, 2048], P(('fsdp', 'tp')), may hold values from -6 to 6
- seq_lengths: int32 [32, 4], P('fsdp'), may hold values from 0 to 512, as said below
- norms: float32 [4, 2048], P(None, ('fsdp', 'tp')), may hold values from -1.2 to 2.72, as said below
- w_qkv: bfloat16 [3, 2048, 2048], P(None, 'fsdp', 'tp'), may hold values from -0.125 to 0.125
- qkv_bias: bfloat16 [3, 32, 64], P(None, 'tp', 'fsdp'), may hold values from -2.5 to 2.5
- w_out: bfloat16 [2048, 2048], P('tp', 'fsdp'), may hold values from -0.75 to 0.75
- w_gate_up: bfloat16 [2, 2048, 5632], P(None, 'fsdp', 'tp'), may hold values from -0.125 to 0.125
- w_down: bfloat16 [5632, 2048], P('tp', 'fsdp'), may hold values from -0.078125 to 0.078125
- out_grad: bfloat16 [16384, 2048], P(('fsdp', 'tp')), may hold values from -24 to 24
Outputs:
- layer_out: bfloat16 [16384, 2048], P(('fsdp', 'tp'))
- grad_tokens: bfloat16 [16384, 2048], P(('fsdp', 'tp'))
- grad_norms: float32 [4, 2048], P(None, ('fsdp', 'tp'))
- grad_qkv: float32 [3, 2048, 2048], P(None, 'fsdp', 'tp')
- grad_bias: float32 [3, 32, 64], P(None, 'tp', 'fsdp')
- grad_out_proj: float32 [2048, 2048], P('tp', 'fsdp')
- grad_gate_up: float32 [2, 2048, 5632], P(None, 'fsdp', 'tp')
- grad_down: float32 [5632, 2048], P('tp', 'fsdp')
The draws below stay inside these ranges and needn't reach their ends.
Inputs may be any that keep to these rules, and one draw needn't show every extreme that they name: `seq_lengths`: in each group the 4 lengths sum to 512; zeros are empty slots. The second sequence of every group starts within the group's first 65 tokens and ends within its last 128; in one group it fills all 512 tokens. `norms`: rows 0 and 2 are positive gains, rows 1 and 3 biases.
All inputs are finite; a program needn't handle non-finite values.
Results may differ from the reference program's by a relative error of at most 0.035.
Values may be sent and summed in bfloat16 or wider, within the bound.
No kernel may reach another device: no remote copies, remote signals or barrier semaphores. Data moves between devices by JAX's collectives and lax.ppermute only.
A program may use at most 192 MiB of HBM per device.

```python
import math
import jax
import jax.numpy as jnp
from jax import lax

D = 2048
HEADS = 32
HD = 64
FF = 5632
ROT = 16
TOK_DEV = 128
GROUP = 512
GROUPS = 32
TOKENS = 16384


def draw_seq_lengths(key, part):
    key = jax.random.fold_in(key, 9)
    keys = jax.random.split(key, 4)
    lead = jax.random.randint(keys[0], (GROUPS,), 0, TOK_DEV // 2 + 1)
    finish = GROUP - TOK_DEV + 1 + jax.random.randint(keys[1], (GROUPS,), 0, TOK_DEV)
    whole = jax.random.randint(keys[2], (), 0, GROUPS)
    chosen = jnp.arange(GROUPS) == whole
    lead = jnp.where(chosen, 0, lead)
    finish = jnp.where(chosen, GROUP, finish)
    remain = GROUP - finish
    split_at = jax.random.randint(keys[3], (GROUPS,), 0, remain + 1)
    return jnp.stack([lead, finish - lead, split_at, remain - split_at], axis=1).astype(jnp.int32)


def draw_norms(key, part):
    key = jax.random.fold_in(key, 5)
    first_key, second_key = jax.random.split(key)
    spread = jax.random.uniform(first_key, (2, D), jnp.float32, -0.7, 0.7)
    shifts = jnp.clip(0.3 * jax.random.normal(second_key, (2, D), jnp.float32), -1.2, 1.2)
    gains = jnp.exp(spread)
    return jnp.stack([gains[0], shifts[0], gains[1], shifts[1]]).astype(jnp.float32)


def with_spikes(array, key, source, target, shards_of, factor):
    def block_of(dim):
        return (jnp.arange(array.shape[dim]) // (array.shape[dim] // shards_of)).reshape((-1,) + (1,) * (array.ndim - 1 - dim))

    first = jax.random.permutation(key, shards_of)[block_of(target)]
    second = (block_of(target) + shards_of // 2) % shards_of
    return jnp.where((block_of(source) == first) | (block_of(source) == second), factor * array, array)


def levels(stream_key, extent, shards, least, top_value):
    def one(axis_at, parts):
        heights = jax.random.uniform(jax.random.fold_in(jax.random.fold_in(stream_key, 6), axis_at), (parts,), jnp.float32, least / len(shards), top_value / len(shards))
        return jnp.repeat(jnp.exp(heights), extent[axis_at] // parts).reshape((-1,) + (1,) * (len(extent) - axis_at - 1))

    factor_of = one(*shards[0])
    for cut in shards[1:]:
        factor_of = factor_of * one(*cut)
    return factor_of


def gaussian(rng, extent, scale, bound, cuts=(), kind=jnp.bfloat16):
    values = scale * jax.random.normal(rng, extent, jnp.float32)
    if cuts:
        values = values * levels(rng, extent, cuts, -0.22, 0.18)
    return jnp.clip(values, -bound, bound).astype(kind)


def heavy_noise(key, extent, scale, most, cuts, heavy, kind=jnp.bfloat16):
    drawn = scale * jax.random.normal(key, extent, jnp.float32)
    if cuts:
        drawn = drawn * levels(key, extent, cuts, -0.22, 0.18)
    return jnp.clip(with_spikes(drawn, jax.random.fold_in(key, 3), *heavy), -most, most).astype(kind)


def setup_inputs(seed: int = 0) -> dict:
    streams_of = jax.random.split(jax.random.key(seed), 10)
    tokens = gaussian(streams_of[0], (TOKENS, D), 1.0, 6.0, ((0, 128),))
    seq_lengths = draw_seq_lengths(jax.random.fold_in(streams_of[9], 71), 0)
    norms = draw_norms(jax.random.fold_in(streams_of[9], 71), 0)
    w_qkv = gaussian(streams_of[3], (3, D, D), D ** -0.5, 0.125, ((1, 32), (2, 4)))
    qkv_bias = gaussian(streams_of[4], (3, HEADS, HD), 0.5, 2.5, ((1, 4), (2, 32)))
    w_out = gaussian(streams_of[5], (D, D), (D // 32) ** -0.5, 0.75, ((0, 4), (1, 32)))
    w_gate_up = gaussian(streams_of[6], (2, D, FF), D ** -0.5, 0.125, ((1, 32), (2, 4)))
    w_down = gaussian(streams_of[7], (FF, D), FF ** -0.5, 0.078125, ((0, 4), (1, 32)))
    out_grad = heavy_noise(streams_of[8], (TOKENS, D), 1.0, 24.0, ((0, 128),), (0, 1, 128, 5.5))
    return {"tokens": tokens, "seq_lengths": seq_lengths, "norms": norms, "w_qkv": w_qkv, "qkv_bias": qkv_bias, "w_out": w_out, "w_gate_up": w_gate_up, "w_down": w_down, "out_grad": out_grad}


@jax.custom_vjp
def low(v):
    return lax.optimization_barrier(v.astype(jnp.bfloat16)).astype(jnp.float32)

@jax.custom_vjp
def low_back(v):
    return v

def low_keep(v):
    return (low(v), None)

def low_pass(kept, grad):
    return (grad,)

def back_keep(v):
    return (v, None)

def back_low(kept, grad):
    return (low(grad),)
low.defvjp(low_keep, low_pass)
low_back.defvjp(back_keep, back_low)
epsilon = 1e-05
highest = lax.Precision.HIGHEST

def layer_norm(values, gain, shift):
    centre = lax.optimization_barrier(jnp.mean(values, axis=-1, keepdims=True))
    centred = values - centre
    spread = lax.optimization_barrier(jnp.mean(centred * centred, axis=-1, keepdims=True))
    return centred * lax.rsqrt(spread + epsilon) * gain + shift

def rotate(values, cosine, sine):
    half = cosine.shape[-1]
    lower = values[..., :half]
    upper = values[..., half:2 * half]
    remain = values[..., 2 * half:]
    return jnp.concatenate([lower * cosine - upper * sine, upper * cosine + lower * sine, remain], axis=-1)

def sequence_marks(lengths, group):
    lengths = lengths.astype(jnp.int32)
    ends = jnp.cumsum(lengths).astype(jnp.int32)
    places = jnp.arange(group, dtype=jnp.int32)
    segment = lax.optimization_barrier(jnp.sum((places[:, None] >= ends[None, :]).astype(jnp.int32), axis=1)).astype(jnp.int32)
    starts = ends - lengths
    slot_ids = jnp.arange(lengths.shape[0], dtype=jnp.int32)
    begin = lax.optimization_barrier(jnp.sum(jnp.where(slot_ids[None, :] == segment[:, None], starts[None, :], 0), axis=1)).astype(jnp.int32)
    return (segment, places - begin)

def rotary_tables(position, width):
    steps = jnp.arange(width // 2, dtype=jnp.float32)
    rates = jnp.exp(steps * (-2.0 * math.log(10000.0) / width))
    angles = position.astype(jnp.float32)[:, None] * rates[None, :]
    return (jnp.cos(angles), jnp.sin(angles))

def head_attention(allowed, items):
    query, keys, values = items
    scores = low_back(jnp.dot(query, keys.T, precision=highest) * (1.0 / math.sqrt(HD)))
    scores = jnp.where(allowed, scores, -1e+30)
    probs = low(jax.nn.softmax(scores, axis=-1))
    return jnp.dot(probs, values, precision=highest)

def group_layer(inputs, lengths, params):
    norms, w_qkv, qkv_bias, w_out, w_gate_up, w_down = params
    group = inputs.shape[0]
    segment, position = sequence_marks(lengths, group)
    places = jnp.arange(group, dtype=jnp.int32)
    allowed = (segment[:, None] == segment[None, :]) & (places[None, :] <= places[:, None])
    cosine, sine = rotary_tables(position, ROT)
    first = low(layer_norm(inputs, norms[0], norms[1]))
    proj = jnp.einsum('rd,cde->cre', first, w_qkv, precision=highest) + qkv_bias.reshape(3, 1, D)
    proj = low_back(proj)
    proj = proj.reshape(3, group, HEADS, HD).transpose(0, 2, 1, 3)
    query = low(rotate(proj[0], cosine, sine))
    keys = low(rotate(proj[1], cosine, sine))
    values = low(proj[2])
    run_head = jax.checkpoint(lambda items: head_attention(allowed, items))
    mixed = lax.map(run_head, (query, keys, values))
    mixed = low_back(low(mixed.transpose(1, 0, 2).reshape(group, D)))
    branch = low_back(jnp.dot(mixed, w_out, precision=highest))
    middle = inputs + branch
    second = low(layer_norm(middle, norms[2], norms[3]))
    gate = low_back(jnp.dot(second, w_gate_up[0], precision=highest))
    upper = low_back(jnp.dot(second, w_gate_up[1], precision=highest))
    hidden = low(jax.nn.silu(gate) * upper)
    branch_two = low_back(jnp.dot(hidden, w_down, precision=highest))
    return middle + branch_two

def forward(inputs, seq_lengths, params):
    grouped = inputs.reshape(GROUPS, GROUP, D)
    run_group = jax.checkpoint(group_layer)
    result = lax.map(lambda items: run_group(items[0], items[1], params), (grouped, seq_lengths))
    return result.reshape(TOKENS, D)

def reference(tokens, seq_lengths, norms, w_qkv, qkv_bias, w_out, w_gate_up, w_down, out_grad):
    params = (norms.astype(jnp.float32), w_qkv.astype(jnp.float32), qkv_bias.astype(jnp.float32), w_out.astype(jnp.float32), w_gate_up.astype(jnp.float32), w_down.astype(jnp.float32))

    def run_layer(inputs, weights):
        return forward(inputs, seq_lengths, weights)
    result, pull = jax.vjp(run_layer, tokens.astype(jnp.float32), params)
    grad_in, grads = pull(out_grad.astype(jnp.float32))
    return (result.astype(jnp.bfloat16), grad_in.astype(jnp.bfloat16), grads[0], grads[1], grads[2], grads[3], grads[4], grads[5])
```

```python
import math

import jax
import jax.numpy as jnp
from jax import lax
from jax.experimental import pallas as pl
from jax.experimental.pallas import tpu as pltpu
from jax.sharding import Mesh, PartitionSpec as P

HD = 64
ROT = 16
EPS = 1e-05
ROWS = 128
FSDP = ("x", "core", "z")
ALL = ("x", "yl", "z", "yh", "core")
BF = jnp.bfloat16
F32 = jnp.float32


def swap(v):
    return lax.ppermute(v, ("yl", "core"), [(0, 0), (1, 2), (2, 1), (3, 3)])


def ring_index(y):
    return (y % 2) * 2 + (y // 2) % 2


def shift(v, k):
    return lax.ppermute(v, ("yl", "yh"), [(ring_index(y), ring_index((y + k) % 4)) for y in range(4)])


def spread_pairs(k):
    pairs = []
    for g in range(2):
        for yh in range(2):
            for c in range(2):
                y = (2 * yh + c + k) % 4
                pairs.append((g * 4 + yh * 2 + c, (y % 2) * 4 + (y // 2) * 2 + g))
    return pairs


def spread(v, k):
    return lax.ppermute(v, ("yl", "yh", "core"), spread_pairs(k))


def collect(v, k):
    return lax.ppermute(v, ("yl", "yh", "core"), [(b, a) for a, b in spread_pairs(k)])


def gather_rows(piece, name):
    with jax.named_scope(name):
        return [piece] + [shift(piece, k) for k in (1, 2, 3)]


def spread_rows(piece, name):
    with jax.named_scope(name):
        return [spread(piece, k) for k in range(4)]


def scatter_rows(blocks, name):
    with jax.named_scope(name):
        return [blocks[0]] + [shift(blocks[k], -k) for k in (2, 1, 3)]


def collect_rows(blocks, name):
    with jax.named_scope(name):
        return [collect(blocks[k], k) for k in (2, 1, 3, 0)]


def call(kernel, args, outs, deps=(), limit=60, grid=None, specs=None, out_specs=None, scratch=()):
    n, m = len(args), len(deps)
    whole = pl.BlockSpec(memory_space=pltpu.VMEM)
    return pl.pallas_call(
        lambda *refs: kernel(*refs[:n], *refs[n + m :]),
        name=kernel.__name__,
        **({} if grid is None else {"grid": grid}),
        in_specs=list(specs or [whole] * n) + [pl.BlockSpec(memory_space=pl.ANY)] * m,
        out_specs=list(out_specs or [whole] * len(outs)),
        out_shape=[jax.ShapeDtypeStruct(s, t) for s, t in outs],
        scratch_shapes=list(scratch),
        compiler_params=pltpu.CompilerParams(vmem_limit_bytes=limit << 20),
    )(*args, *deps)


def hold(arrays, deps):
    n, m = len(arrays), len(deps)
    return pl.pallas_call(
        lambda *refs: None,
        name="hold",
        in_specs=[pl.BlockSpec(memory_space=pl.ANY)] * (n + m),
        out_specs=[pl.BlockSpec(memory_space=pl.ANY)] * n,
        out_shape=[jax.ShapeDtypeStruct(v.shape, v.dtype) for v in arrays],
        input_output_aliases={i: i for i in range(n)},
    )(*arrays, *deps)


MM = (((1,), (0,)), ((), ()))
MT = (((1,), (1,)), ((), ()))
TM = (((0,), (0,)), ((), ()))


def mul(a, b, dims):
    return lax.dot_general(a, b, dims, preferred_element_type=F32)


def total(refs):
    value = refs[0][...].astype(F32)
    for ref in refs[1:]:
        value = value + ref[...].astype(F32)
    return value


def normal_kernel(tokens, n):
    n[...] = normal(tokens[...].astype(F32))[0].astype(BF)


def middle_kernel(tokens, norms, *refs):
    middle = tokens[...].astype(F32) + total(refs[:4])
    refs[4][...] = middle
    refs[6][...] = middle.astype(BF)
    refs[5][...] = (normal(middle)[0] * norms[2:3] + norms[3:4]).astype(BF)


def back_kernel(middle, norms, grad, *refs):
    n, r = normal(middle[...])
    part = total(refs[:4])
    value = grad[...].astype(F32) + normal_back(n, r, part * norms[2:3])
    refs[4][...] = value.astype(BF)
    refs[5][0:1] = jnp.sum(part * n, axis=0, keepdims=True)
    refs[5][1:2] = jnp.sum(part, axis=0, keepdims=True)


def tokens_kernel(tokens, norms, grad, *refs):
    n, r = normal(tokens[...].astype(F32))
    refs[4][...] = (grad[...].astype(F32) + normal_back(n, r, total(refs[:4]) * norms[0:1])).astype(BF)


def last_kernel(middle, *refs):
    refs[4][...] = (middle[...].astype(F32) + total(refs[:4])).astype(BF)


def block_shapes(own=F32):
    return [((ROWS, 2048), own)] + [((ROWS, 2048), BF)] * 3


def store_blocks(value, refs, columns):
    for j in range(4):
        refs[j][:, columns] = value[j * ROWS : (j + 1) * ROWS].astype(refs[j].dtype)


def mask_of(begin, place, row):
    return jnp.where((row[...] >= begin[...]) & (row[...] <= place[...]), 0.0, -1e30).astype(F32)


def lane_of(width):
    return lax.broadcasted_iota(jnp.int32, (1, width), 1)


def turn(v, tables, sign):
    straight, ahead, behind = tables
    return v * straight[...] + sign * (pltpu.roll(v, 120, 1) * ahead[...] + pltpu.roll(v, 8, 1) * behind[...])


def attend_kernel(n0, n1, n2, n3, norms, wq, wk, wv, wo, bias, straight, ahead, behind, begin, place, row, *refs):
    first, query, keys, values, logs, mixed, t0, t1, t2, t3, mask = refs
    step = pl.program_id(0)

    @pl.when(step == 0)
    def _():
        for j, n in enumerate((n0, n1, n2, n3)):
            first[j * ROWS : (j + 1) * ROWS] = (n[...].astype(F32) * norms[0:1] + norms[1:2]).astype(BF)
        mask[...] = mask_of(begin, place, row)
        logs[...] = jnp.zeros_like(logs)

    tables = (straight, ahead, behind)
    q4 = mul(first[...], wq[...], MM) + bias[0, pl.ds(step, 1)]
    k4 = mul(first[...], wk[...], MM) + bias[1, pl.ds(step, 1)]
    v4 = (mul(first[...], wv[...], MM) + bias[2, pl.ds(step, 1)]).astype(BF)
    lane = lane_of(128)
    for pair in range(2):
        at = slice(pair * 128, (pair + 1) * 128)
        columns = pl.ds(pl.multiple_of(step * 256 + pair * 128, 128), 128)
        q = (turn(q4[:, at], tables, 1.0).astype(BF) * BF(1.0 / math.sqrt(HD))).astype(BF)
        k = turn(k4[:, at], tables, 1.0).astype(BF)
        v = v4[:, at]
        query[:, columns] = q
        keys[:, columns] = k
        values[:, columns] = v
        result = None
        for head in range(2):
            own = (lane >= 64) if head else (lane < 64)
            scores = mul(jnp.where(own, q, BF(0)), k, MT) + mask[...]
            top = jnp.max(scores, axis=1, keepdims=True)
            shifted = jnp.exp(scores - top)
            whole = jnp.sum(shifted, axis=1, keepdims=True)
            probs = (shifted * (1.0 / whole)).astype(BF)
            out = mul(probs, v, MM)
            result = out if result is None else jnp.where(own, out, result)
            logs[...] = jnp.where(lane == step * 4 + pair * 2 + head, top + jnp.log(whole), logs[...])
        mixed[:, columns] = result.astype(BF)

    @pl.when(step == 1)
    def _():
        for i in range(4):
            columns = slice(i * 512, (i + 1) * 512)
            store_blocks(mul(mixed[...], wo[columns], MT), (t0, t1, t2, t3), columns)


def attend_back_kernel(g0, g1, g2, g3, wo, query, keys, values, logs, straight, ahead, behind, begin, place, row, *refs):
    grad_proj, grad_bias, mask, grad_mixed = refs
    step = pl.program_id(0)

    @pl.when(step == 0)
    def _():
        for j, g in enumerate((g0, g1, g2, g3)):
            grad_mixed[j * ROWS : (j + 1) * ROWS] = mul(g[...], wo[...], MM).astype(BF)
        mask[...] = mask_of(begin, place, row)

    tables = (straight, ahead, behind)
    lane = lane_of(128)
    columns = pl.ds(pl.multiple_of(step * 128, 128), 128)
    q, k, v, g = query[...], keys[...], values[...], grad_mixed[:, columns]
    grad_q = grad_k = grad_v = 0.0
    for head in range(2):
        own = (lane >= 64) if head else (lane < 64)
        q1, k1, g1 = (jnp.where(own, w, BF(0)) for w in (q, k, g))
        log = jnp.sum(jnp.where(lane == step * 2 + head, logs[...], 0.0), axis=1, keepdims=True)
        probs = jnp.exp(mul(q1, k, MT) + mask[...] - log)
        grad_probs = mul(g1, v, MT)
        inner = jnp.sum(grad_probs * probs, axis=1, keepdims=True)
        grad_scores = (probs * (grad_probs - inner)).astype(BF)
        grad_q = grad_q + mul(grad_scores, k1, MM)
        grad_k = grad_k + mul(grad_scores, q1, TM)
        grad_v = grad_v + mul(probs.astype(BF), g1, TM)
    for c, value in enumerate(
        (turn(grad_q * (1.0 / math.sqrt(HD)), tables, -1.0), turn(grad_k, tables, -1.0), grad_v)
    ):
        low = value.astype(BF)
        at = pl.ds(pl.multiple_of(c * 512 + step * 128, 128), 128)
        grad_proj[:, at] = low
        sums = jnp.sum(low.astype(F32), axis=0, keepdims=True)
        grad_bias[pl.ds(c * 8 + 2 * step, 1)] = sums[:, :HD]
        grad_bias[pl.ds(c * 8 + 2 * step + 1, 1)] = sums[:, HD:]


def feed_kernel(*refs):
    second, grads, w, (hidden, pair, t0, t1, t2, t3, held, sems) = refs[:4], refs[4:8], refs[8], refs[9:]
    cuts = [(i * 256, 256) for i in range(5)] + [(1280, 128)]
    copies = []
    for i, (f, width) in enumerate(cuts):
        for c, at, size in ((0, 2 * f, 2 * width), (1, 2816 + f, width)):
            copy = pltpu.make_async_copy(w.at[:, at : at + size], held.at[:, at : at + size], sems.at[i, c])
            copy.start()
            copies.append(copy)
    for i, (f, width) in enumerate(cuts):
        copies[2 * i].wait()
        copies[2 * i + 1].wait()
        for j in range(2):
            rows = slice(j * 256, (j + 1) * 256)
            lhs = jnp.concatenate([second[2 * j][...], second[2 * j + 1][...]], axis=0)
            both = mul(lhs, held[:, 2 * f : 2 * (f + width)], MM)
            lhs = jnp.concatenate([grads[2 * j][...], grads[2 * j + 1][...]], axis=0)
            back = mul(lhs, held[:, 2816 + f : 2816 + f + width], MM)
            for b in range(width // 128):
                gate, up = both[:, b * 256 : b * 256 + 128], both[:, b * 256 + 128 : b * 256 + 256]
                grad = back[:, b * 128 : (b + 1) * 128]
                sig = jax.nn.sigmoid(gate)
                silu = gate * sig
                at = f + b * 128
                hidden[rows, at : at + 128] = (silu * up).astype(BF)
                pair[rows, 2 * at : 2 * at + 128] = (grad * up * (sig + silu * (1.0 - sig))).astype(BF)
                pair[rows, 2 * at + 128 : 2 * at + 256] = (grad * silu).astype(BF)
    for i in range(4):
        columns = slice(i * 512, (i + 1) * 512)
        store_blocks(mul(pair[...], held[columns, :2816], MT), (t0, t1, t2, t3), columns)


def outer_kernel(a0, a1, a2, a3, b, c0, c1, c2, c3, d, out):
    n, m = b.shape[1], d.shape[1]
    a = jnp.concatenate([a0[...], a1[...], a2[...], a3[...]], axis=0)
    c = jnp.concatenate([c0[...], c1[...], c2[...], c3[...]], axis=0)
    out[:, :n] = mul(a, b[...], TM).astype(BF)
    out[:, n : n + m] = mul(c, d[...], TM).astype(BF)


def outer(a, b, c, d, deps=(), tile=256):
    n, m = b.shape[1], d.shape[1]
    left = [pl.BlockSpec((ROWS, tile), lambda i: (0, i))] * 4
    whole = lambda w: pl.BlockSpec((512, w), lambda i: (0, 0))
    return call(
        outer_kernel,
        (*a, b, *c, d),
        [((2048, n + m), BF)],
        deps,
        grid=(2048 // tile,),
        specs=left + [whole(n)] + left + [whole(m)],
        out_specs=[pl.BlockSpec((tile, n + m), lambda i: (i, 0))],
    )[0]


def half_columns(a, b, c, d, extra):
    n, m = b.shape[1], d.shape[1]
    rows = jnp.concatenate([ref[...] for ref in c], axis=0)
    return ((0, n, mul(a[...], b[...], TM)), (n, m, mul(rows, d[...], TM)), (n + m, extra.shape[1], extra[...].astype(F32)))


def their_half_kernel(place, a, b, c0, c1, c2, c3, d, extra, out):
    for begin, width, value in half_columns(a, b, (c0, c1, c2, c3), d, extra):
        out[:, begin : begin + width] = value.astype(BF)


def own_half_kernel(place, a, b, c0, c1, c2, c3, d, extra, theirs, one, two):
    split = one.shape[-1]
    for begin, width, value in half_columns(a, b, (c0, c1, c2, c3), d, extra):
        value = (value + theirs[:, begin : begin + width].astype(F32)).astype(BF)
        for z in range(4):
            at = lax.rem(z - place[2] + 4, 4)
            rows = value[z * 64 : (z + 1) * 64]
            if begin < split:
                one[0, at] = rows[:, :split]
                two[at, 0, :, : width - split] = rows[:, split:]
            else:
                two[at, 0, :, begin - split : begin - split + width] = rows


def outer_half(place, a, b, c, d, extra, split, deps, theirs=None):
    rows = a.shape[0]
    n, m, e = b.shape[1], d.shape[1], extra.shape[1]
    wide = n + m + e
    pick = lambda i, p: 2 * lax.rem(p[1] + i, 4) + p[0]
    left = pl.BlockSpec((rows, 256), lambda i, p: (0, pick(i, p)))
    quarter = [pl.BlockSpec((ROWS, 256), lambda i, p: (0, pick(i, p)))] * 4
    whole = lambda w: pl.BlockSpec((rows, w), lambda i, p: (0, 0))
    flat = pl.BlockSpec((256, wide), lambda i, p: (i, 0))
    specs = [left, whole(n), *quarter, whole(m), pl.BlockSpec((256, e), lambda i, p: (pick(i, p), 0))]
    if theirs is None:
        kernel, args, outs, shapes = their_half_kernel, [], [flat], [(1024, wide)]
    else:
        kernel, args, specs = own_half_kernel, [theirs], specs + [flat]
        outs = [
            pl.BlockSpec((1, 4, 64, split), lambda i, p: (i, 0, 0, 0)),
            pl.BlockSpec((4, 1, 64, wide - split), lambda i, p: (0, i, 0, 0)),
        ]
        shapes = [(4, 4, 64, split), (4, 4, 64, wide - split)]
    count = 1 + len(specs)
    return pl.pallas_call(
        lambda *refs: kernel(*refs[:count], *refs[count + len(deps) :]),
        name=kernel.__name__,
        grid_spec=pltpu.PrefetchScalarGridSpec(
            num_scalar_prefetch=1,
            grid=(4,),
            in_specs=specs + [pl.BlockSpec(memory_space=pl.ANY)] * len(deps),
            out_specs=outs,
        ),
        out_shape=[jax.ShapeDtypeStruct(shape, BF) for shape in shapes],
        compiler_params=pltpu.CompilerParams(vmem_limit_bytes=60 << 20),
    )(place, a, b, *c, d, extra, *args, *deps)


def term_kernel(a, w, *refs):
    value = mul(a[...], w[...], MT)
    if len(refs) > 4:
        *n, norm_two, grad_bias, t0, t1, t2, t3, tail = refs
        refs = (t0, t1, t2, t3)
        gain = jnp.zeros((1, value.shape[1]), F32)
        for j in range(4):
            gain = gain + jnp.sum(value[j * ROWS : (j + 1) * ROWS] * n[j][...].astype(F32), axis=0, keepdims=True)
        rows = jnp.concatenate([gain, jnp.sum(value, axis=0, keepdims=True), norm_two[...], jnp.zeros_like(norm_two), jnp.zeros_like(norm_two)], axis=0)
        step = pl.program_id(0)
        bias = jnp.zeros((24, 128), F32)
        lane = lane_of(HD)
        for f in range(8):
            ones = [jnp.sum(jnp.where(lane == 2 * (step * 8 + f) + j, grad_bias[...], 0.0), axis=1, keepdims=True) for j in (0, 1)]
            bias = jnp.concatenate(ones + [jnp.zeros((24, 126), F32)], axis=1)
            tail[f * 64 : (f + 1) * 64] = jnp.concatenate(
                [
                    jnp.concatenate([rows[:, f * 64 : (f + 1) * 64], jnp.zeros((8, 64), F32)], axis=1),
                    bias,
                    jnp.zeros((32, 128), F32),
                ],
                axis=0,
            ).astype(BF)
    for j in range(4):
        refs[j][...] = value[j * ROWS : (j + 1) * ROWS].astype(refs[j].dtype)


def row_term(a, w, at, n=None, norm_two=None, grad_bias=None, deps=(), own=BF, tile=512):
    rows, depth = a.shape
    block = pl.BlockSpec((ROWS, tile), lambda i: (0, i))
    args = [a, w]
    specs = [pl.BlockSpec((rows, depth), lambda i: (0, 0)), pl.BlockSpec((tile, depth), lambda i: (i, at))]
    shapes, outs = block_shapes(own), [block] * 4
    if n is not None:
        args += [*n, norm_two, grad_bias]
        specs += [block] * 4 + [pl.BlockSpec((2, tile), lambda i: (0, i)), pl.BlockSpec((24, HD), lambda i: (0, 0))]
        shapes = shapes + [((2048, 128), BF)]
        outs = outs + [pl.BlockSpec((tile, 128), lambda i: (i, 0))]
    return call(term_kernel, args, shapes, deps, grid=(2048 // tile,), specs=specs, out_specs=outs)


def along(v, axis, k):
    return lax.ppermute(v, axis, [(i, (i + k) % 4) for i in range(4)])


def sum_along(blocks, axis, name):
    with jax.named_scope(name):
        got = [along(blocks[k], axis, k) for k in (2, 1, 3)]
    return blocks[0].astype(F32) + got[0].astype(F32) + got[1].astype(F32) + got[2].astype(F32)


def normal(v):
    centred = v - jnp.mean(v, axis=-1, keepdims=True)
    r = lax.rsqrt(jnp.mean(centred * centred, axis=-1, keepdims=True) + EPS)
    return centred * r, r


def normal_back(n, r, t):
    return r * (t - jnp.mean(t, axis=-1, keepdims=True) - n * jnp.mean(t * n, axis=-1, keepdims=True))


def across(v):
    return lax.ppermute(v, "core", [(0, 1), (1, 0)])


def body(tokens, seq_lengths, norms, w_qkv, qkv_bias, w_out, w_gate_up, w_down, out_grad):
    me = 2 * lax.axis_index("yh") + lax.axis_index("yl")
    small = jnp.concatenate(
        [
            norms,
            qkv_bias.astype(F32).reshape(3, 16),
            jnp.pad(seq_lengths.astype(F32), ((0, 0), (0, 12))),
        ],
        axis=0,
    )
    row_shape = [((ROWS, 2048), BF)]
    w_attn = swap(jnp.concatenate([w_qkv[0], w_qkv[1], w_qkv[2], w_out.T], axis=1))
    n_own = call(normal_kernel, (tokens,), row_shape)[0]
    pieces = [spread(small, k) for k in range(4)]
    lengths = pieces[0][7, :4].astype(jnp.int32)
    bias_row = pieces[0][4:7].reshape(1, 48)
    turned = jnp.stack([p[:4] for p in pieces[::-1]] * 2)
    ordered = lax.dynamic_slice_in_dim(turned, 3 - me, 4, axis=0)
    norm_part = ordered.transpose(1, 0, 2).reshape(4, 64)
    high = norm_part.astype(BF)
    rest = norm_part - high.astype(F32)
    middle_part = rest.astype(BF)
    low = (rest - middle_part.astype(F32)).astype(BF)
    extra = jnp.concatenate([high, middle_part, low, jnp.pad(bias_row.astype(BF), ((0, 0), (0, 16)))], axis=0)
    extra = jnp.pad(extra, ((0, 64 - 13), (0, 64)))
    (extra,) = hold([extra], (n_own,))
    attn_full = lax.all_gather(jnp.concatenate([w_attn, extra], axis=1), FSDP, axis=0, tiled=True)

    n_rows = spread_rows(n_own, "n_rows")
    w_ffn = swap(
        jnp.concatenate([w_gate_up.reshape(2, 64, 11, 128).transpose(1, 2, 0, 3).reshape(64, 2816), w_down.T], axis=1)
    )
    inputs = swap(tokens)
    mlp_rows = spread_rows(out_grad, "grad_rows")
    ffn_full = lax.all_gather(w_ffn, FSDP, axis=0, tiled=True)

    extras = attn_full[:, 2048:].reshape(32, 64, 128)
    norm_all = extras[:, :12, :64].astype(F32).reshape(32, 3, 4, 64).sum(axis=1)
    norm_all = norm_all.transpose(1, 0, 2).reshape(4, 2048)
    bias = extras[:, 12, :48].astype(F32).reshape(32, 3, 8, 2).transpose(1, 2, 0, 3).reshape(3, 2, 256)

    places = (((me - jnp.arange(4, dtype=jnp.int32)) % 4) * ROWS)[:, None] + jnp.arange(ROWS, dtype=jnp.int32)
    places = places.reshape(512)
    ends = jnp.cumsum(lengths)
    segment = jnp.sum((places[:, None] >= ends[None, :]).astype(jnp.int32), axis=1)
    begin = jnp.sum(
        jnp.where(jnp.arange(4, dtype=jnp.int32)[None, :] == segment[:, None], (ends - lengths)[None, :], 0), axis=1
    )
    position = places - begin
    rates = jnp.exp(jnp.arange(ROT // 2, dtype=F32) * (-2.0 * math.log(10000.0) / ROT))
    angles = position.astype(F32)[:, None] * rates[None, :]
    cosine, sine = jnp.cos(angles), jnp.sin(angles)
    zero, one = jnp.zeros((512, 8), F32), jnp.ones((512, 48), F32)
    still = jnp.zeros((512, 48), F32)
    tables = (
        jnp.concatenate([cosine, cosine, one] * 2, axis=1),
        jnp.concatenate([-sine, zero, still] * 2, axis=1),
        jnp.concatenate([zero, sine, still] * 2, axis=1),
    )
    marks = (begin[:, None], places[:, None], places[None, :])

    sticky = lambda *shape: pl.BlockSpec(shape, lambda i: (0,) * len(shape))
    part = lambda first: pl.BlockSpec((2048, 256), lambda i: (0, first + i))
    table_specs = [sticky(512, 128)] * 3 + [sticky(512, 1)] * 2 + [sticky(1, 512)]
    first, query, keys, values, logs, mixed, *term = call(
        attend_kernel,
        (*n_rows, norm_all, *[attn_full] * 4, bias, *tables, *marks),
        [((512, 2048), BF)] + [((512, 512), BF)] * 3 + [((512, 128), F32), ((512, 512), BF)] + block_shapes(),
        (w_ffn, inputs),
        grid=(2,),
        specs=[sticky(ROWS, 2048)] * 4
        + [sticky(4, 2048), part(0), part(2), part(4), pl.BlockSpec((2048, 512), lambda i: (0, 3)), sticky(3, 2, 256)]
        + table_specs,
        out_specs=[sticky(512, 2048)]
        + [sticky(512, 512)] * 3
        + [sticky(512, 128), sticky(512, 512)]
        + [sticky(ROWS, 2048)] * 4,
        scratch=[pltpu.VMEM((512, 512), F32)],
    )
    term = hold(term, mlp_rows)
    middle, second, middle_low = call(
        middle_kernel, (inputs, norm_all, *scatter_rows(term, "attn_sum")), [((ROWS, 2048), F32)] + row_shape * 2
    )
    second = gather_rows(second, "second_rows")
    middle_low = swap(hold([middle_low], second)[0])
    hidden, grad_pair, *term = call(
        feed_kernel,
        (*second, *mlp_rows, ffn_full),
        [((512, 1408), BF), ((512, 2816), BF)] + block_shapes(),
        specs=[pl.BlockSpec(memory_space=pltpu.VMEM)] * 8 + [pl.BlockSpec(memory_space=pl.ANY)],
        scratch=[pltpu.VMEM((2048, 4224), BF), pltpu.SemaphoreType.DMA((6, 2))],
    )
    term = scatter_rows(term, "second_sum")
    grad_ffn = outer(second, grad_pair, mlp_rows, hidden)
    last_term = row_term(hidden, ffn_full, 2, deps=(grad_ffn,))
    grad_rows, norm_two = call(
        back_kernel,
        (middle, norm_all, mlp_rows[0], *term),
        row_shape + [((2, 2048), F32)],
        (last_term[0],),
    )
    (grad_ffn,) = hold([grad_ffn], (grad_rows,))
    ffn_sum = swap(lax.psum_scatter(grad_ffn, FSDP, scatter_dimension=0, tiled=True)).astype(F32)
    attn_rows = gather_rows(grad_rows, "middle_rows")
    *last_term, grad_middle = hold([*last_term, grad_rows], attn_rows[1:])
    last_term = collect_rows(last_term, "out_sum")
    grad_middle = swap(grad_middle)
    column = pl.BlockSpec((512, 128), lambda i: (0, i))
    grad_proj, grad_bias = call(
        attend_back_kernel,
        (*attn_rows, attn_full, query, keys, values, logs, *tables, *marks),
        [((512, 1536), BF), ((24, HD), F32)],
        grid=(4,),
        specs=[sticky(ROWS, 2048)] * 4
        + [pl.BlockSpec((2048, 512), lambda i: (0, 3)), column, column, column, sticky(512, 128)]
        + table_specs,
        out_specs=[sticky(512, 1536), sticky(24, HD)],
        scratch=[pltpu.VMEM((512, 512), F32), pltpu.VMEM((512, 512), BF)],
    )

    place = jnp.stack([lax.axis_index("core"), lax.axis_index("x"), lax.axis_index("z")]).astype(jnp.int32)
    *term, tail = row_term(grad_proj, attn_full, 0, n_rows, norm_two, grad_bias)
    first_term = collect_rows(hold(term, last_term), "first_sum")
    place_other = place * jnp.array([-1, 1, 1]) + jnp.array([1, 0, 0])
    theirs = across(outer_half(place_other, first, grad_proj, attn_rows, mixed, tail, 1024, last_term)[0])
    one, two = outer_half(place, first, grad_proj, attn_rows, mixed, tail, 1024, first_term, theirs)
    layer_out = call(last_kernel, (middle_low, *last_term), row_shape)[0]
    one = sum_along(one, "x", "one_x").astype(BF)
    two = sum_along(two, "z", "two_z").astype(BF)
    grad_tokens = call(tokens_kernel, (tokens, norm_all, grad_middle, *first_term), row_shape, (one, two))[0]
    one = sum_along(one, "z", "one_z").astype(BF)
    two = sum_along(two, "x", "two_x")
    small = two[:32, 1024:].astype(F32)
    (attn_grads,) = hold([jnp.concatenate([one, two[:, :1024].astype(BF)], axis=1)], (layer_out, grad_tokens))
    attn_grads = swap(attn_grads).astype(F32)

    norm_parts = small[:4, :64].reshape(4, 4, 16).transpose(1, 0, 2)
    pick = lambda k: lax.dynamic_index_in_dim(norm_parts, (me - k) % 4, 0, keepdims=False)
    with jax.named_scope("norm_sum"):
        got = collect(jnp.concatenate([pick(0), small[8:, :2].reshape(3, 16)], axis=0), 0)
        grad_norms = got[:4] + collect(pick(1), 1) + collect(pick(2), 2) + collect(pick(3), 3)
    return (
        layer_out,
        grad_tokens,
        grad_norms,
        attn_grads[:, :1536].reshape(64, 3, 512).transpose(1, 0, 2),
        got[4:].reshape(3, 8, 2),
        attn_grads[:, 1536:2048].T,
        ffn_sum[:, :2816].reshape(64, 11, 2, 128).transpose(2, 0, 1, 3).reshape(2, 64, 1408),
        ffn_sum[:, 2816:].T,
    )


def solution(mesh):
    ring = Mesh(mesh.devices.reshape(4, 2, 4, 2, 2), ALL)
    fsdp, tp = ("x", "yl", "z"), ("yh", "core")
    return jax.shard_map(
        body,
        mesh=ring,
        in_specs=(
            P(ALL, None),
            P(fsdp, None),
            P(None, ALL),
            P(None, fsdp, tp),
            P(None, tp, fsdp),
            P(tp, fsdp),
            P(None, fsdp, tp),
            P(tp, fsdp),
            P(ALL, None),
        ),
        out_specs=(
            P(ALL, None),
            P(ALL, None),
            P(None, ALL),
            P(None, fsdp, tp),
            P(None, tp, fsdp),
            P(tp, fsdp),
            P(None, fsdp, tp),
            P(tp, fsdp),
        ),
        check_vma=False,
    )
```

```python
import math

import jax
import jax.numpy as jnp
from jax import lax
from jax.experimental import pallas as pl
from jax.experimental.pallas import tpu as pltpu
from jax.sharding import Mesh, PartitionSpec as P

HD = 64
ROT = 16
EPS = 1e-05
ROWS = 128
FSDP = ("x", "core", "z")
ALL = ("x", "yl", "z", "yh", "core")
BF = jnp.bfloat16
F32 = jnp.float32


def swap(v):
    return lax.ppermute(v, ("yl", "core"), [(0, 0), (1, 2), (2, 1), (3, 3)])


def ring_index(y):
    return (y % 2) * 2 + (y // 2) % 2


def shift(v, k):
    return lax.ppermute(v, ("yl", "yh"), [(ring_index(y), ring_index((y + k) % 4)) for y in range(4)])


def spread_pairs(k):
    pairs = []
    for g in range(2):
        for yh in range(2):
            for c in range(2):
                y = (2 * yh + c + k) % 4
                pairs.append((g * 4 + yh * 2 + c, (y % 2) * 4 + (y // 2) * 2 + g))
    return pairs


def spread(v, k):
    return lax.ppermute(v, ("yl", "yh", "core"), spread_pairs(k))


def collect(v, k):
    return lax.ppermute(v, ("yl", "yh", "core"), [(b, a) for a, b in spread_pairs(k)])


def gather_rows(piece, name):
    with jax.named_scope(name):
        return [piece] + [shift(piece, k) for k in (1, 2, 3)]


def spread_rows(piece, name):
    with jax.named_scope(name):
        return [spread(piece, k) for k in range(4)]


def scatter_rows(blocks, name):
    with jax.named_scope(name):
        return [blocks[0]] + [shift(blocks[k], -k) for k in (2, 1, 3)]


def collect_rows(blocks, name):
    with jax.named_scope(name):
        return [collect(blocks[k], k) for k in (2, 1, 3, 0)]


def call(kernel, args, outs, deps=(), limit=None, grid=None, specs=None, out_specs=None, scratch=()):
    n, m = len(args), len(deps)
    limit = limit or (60 if grid or scratch else 16)
    whole = pl.BlockSpec(memory_space=pltpu.VMEM)
    return pl.pallas_call(
        lambda *refs: kernel(*refs[:n], *refs[n + m :]),
        name=kernel.__name__,
        **({} if grid is None else {"grid": grid}),
        in_specs=list(specs or [whole] * n) + [pl.BlockSpec(memory_space=pl.ANY)] * m,
        out_specs=list(out_specs or [whole] * len(outs)),
        out_shape=[jax.ShapeDtypeStruct(s, t) for s, t in outs],
        scratch_shapes=list(scratch),
        compiler_params=pltpu.CompilerParams(vmem_limit_bytes=limit << 20),
    )(*args, *deps)


def hold(arrays, deps):
    n, m = len(arrays), len(deps)
    return pl.pallas_call(
        lambda *refs: None,
        name="hold",
        in_specs=[pl.BlockSpec(memory_space=pl.ANY)] * (n + m),
        out_specs=[pl.BlockSpec(memory_space=pl.ANY)] * n,
        out_shape=[jax.ShapeDtypeStruct(v.shape, v.dtype) for v in arrays],
        input_output_aliases={i: i for i in range(n)},
    )(*arrays, *deps)


MM = (((1,), (0,)), ((), ()))
MT = (((1,), (1,)), ((), ()))
TM = (((0,), (0,)), ((), ()))


def mul(a, b, dims):
    return lax.dot_general(a, b, dims, preferred_element_type=F32)


def total(refs):
    value = refs[0][...].astype(F32)
    for ref in refs[1:]:
        value = value + ref[...].astype(F32)
    return value


def pack_kernel(me, w, p0, p1, p2, p3, out):
    out[:, :2048] = w[...]
    norms = jnp.zeros((4, 64), F32)
    for k, piece in enumerate((p0, p1, p2, p3)):
        place = lax.rem(me[0] - k + 4, 4)
        for q in range(4):
            parts = [jnp.zeros((4, 16 * q), F32)] * (q > 0) + [piece[:4]] + [jnp.zeros((4, 48 - 16 * q), F32)] * (q < 3)
            norms = norms + jnp.where(place == q, jnp.concatenate(parts, axis=1), 0.0)
    high = norms.astype(BF).astype(F32)
    middle = (norms - high).astype(BF).astype(F32)
    biases = jnp.concatenate([p0[4:5], p0[5:6], p0[6:7], jnp.zeros((1, 16), F32)], axis=1)
    rows = [high, middle, norms - high - middle, biases, jnp.zeros((51, 64), F32)]
    rows = jnp.concatenate([jnp.concatenate(rows, axis=0), jnp.zeros((64, 64), F32)], axis=1)
    out[:, 2048:] = rows.astype(BF)


def normal_kernel(tokens, n):
    n[...] = normal(tokens[...].astype(F32))[0].astype(BF)


def middle_kernel(tokens, norms, *refs):
    middle = tokens[...].astype(F32) + total(refs[:4])
    refs[4][...] = middle
    refs[5][...] = (normal(middle)[0] * norms[2:3] + norms[3:4]).astype(BF)


def back_kernel(middle, norms, grad, *refs):
    n, r = normal(middle[...])
    part = total(refs[:4])
    value = grad[...].astype(F32) + normal_back(n, r, part * norms[2:3])
    refs[4][...] = value.astype(BF)
    refs[5][0:1] = jnp.sum(part * n, axis=0, keepdims=True)
    refs[5][1:2] = jnp.sum(part, axis=0, keepdims=True)


def tokens_kernel(tokens, norms, grad, *refs):
    n, r = normal(tokens[...].astype(F32))
    refs[2][...] = (grad[...].astype(F32) + normal_back(n, r, total(refs[:2]) * norms[0:1])).astype(BF)


def last_kernel(middle, *refs):
    refs[2][...] = (middle[...] + total(refs[:2])).astype(BF)


def fold_kernel(own, pair, got, mine, theirs):
    mine[...] = own[...].astype(F32) + got[:ROWS].astype(F32)
    theirs[...] = (pair[...].astype(F32) + got[ROWS:].astype(F32)).astype(BF)


def block_shapes(own=F32):
    return [((ROWS, 2048), own)] + [((ROWS, 2048), BF)] * 3


def store_blocks(value, refs, columns):
    for j in range(4):
        refs[j][:, columns] = value[j * ROWS : (j + 1) * ROWS].astype(refs[j].dtype)


def mask_of(begin, place, row):
    return jnp.where((row[...] >= begin[...]) & (row[...] <= place[...]), 0.0, -1e30).astype(F32)


def lane_of(width):
    return lax.broadcasted_iota(jnp.int32, (1, width), 1)


def turn(v, tables, sign):
    straight, ahead, behind = tables
    return v * straight[...] + sign * (pltpu.roll(v, 120, 1) * ahead[...] + pltpu.roll(v, 8, 1) * behind[...])


def attend_kernel(n0, n1, n2, n3, norms, wq, wk, wv, wo, bias, straight, ahead, behind, begin, place, row, *refs):
    first, query, keys, values, logs, mixed, t0, t1, t2, t3, mask = refs
    step = pl.program_id(0)

    @pl.when(step == 0)
    def _():
        for j, n in enumerate((n0, n1, n2, n3)):
            first[j * ROWS : (j + 1) * ROWS] = (n[...].astype(F32) * norms[0:1] + norms[1:2]).astype(BF)
        mask[...] = mask_of(begin, place, row)
        logs[...] = jnp.zeros_like(logs)

    tables = (straight, ahead, behind)
    q4 = mul(first[...], wq[...], MM) + bias[0, pl.ds(step, 1)]
    k4 = mul(first[...], wk[...], MM) + bias[1, pl.ds(step, 1)]
    v4 = (mul(first[...], wv[...], MM) + bias[2, pl.ds(step, 1)]).astype(BF)
    lane = lane_of(128)
    for pair in range(2):
        at = slice(pair * 128, (pair + 1) * 128)
        columns = pl.ds(pl.multiple_of(step * 256 + pair * 128, 128), 128)
        q = (turn(q4[:, at], tables, 1.0).astype(BF) * BF(1.0 / math.sqrt(HD))).astype(BF)
        k = turn(k4[:, at], tables, 1.0).astype(BF)
        v = v4[:, at]
        query[:, columns] = q
        keys[:, columns] = k
        values[:, columns] = v
        result = None
        for head in range(2):
            own = (lane >= 64) if head else (lane < 64)
            scores = mul(jnp.where(own, q, BF(0)), k, MT) + mask[...]
            top = jnp.max(scores, axis=1, keepdims=True)
            shifted = jnp.exp(scores - top)
            whole = jnp.sum(shifted, axis=1, keepdims=True)
            probs = (shifted * (1.0 / whole)).astype(BF)
            out = mul(probs, v, MM)
            result = out if result is None else jnp.where(own, out, result)
            logs[...] = jnp.where(lane == step * 4 + pair * 2 + head, top + jnp.log(whole), logs[...])
        mixed[:, columns] = result.astype(BF)

    @pl.when(step == 1)
    def _():
        for i in range(4):
            columns = slice(i * 512, (i + 1) * 512)
            store_blocks(mul(mixed[...], wo[columns], MT), (t0, t1, t2, t3), columns)


def attend_back_kernel(g0, g1, g2, g3, wo, query, keys, values, logs, straight, ahead, behind, begin, place, row, *refs):
    grad_proj, grad_bias, mask, grad_mixed = refs
    step = pl.program_id(0)

    @pl.when(step == 0)
    def _():
        for j, g in enumerate((g0, g1, g2, g3)):
            grad_mixed[j * ROWS : (j + 1) * ROWS] = mul(g[...], wo[...], MM).astype(BF)
        mask[...] = mask_of(begin, place, row)

    tables = (straight, ahead, behind)
    lane = lane_of(128)
    columns = pl.ds(pl.multiple_of(step * 128, 128), 128)
    q, k, v, g = query[...], keys[...], values[...], grad_mixed[:, columns]
    grad_q = grad_k = grad_v = 0.0
    for head in range(2):
        own = (lane >= 64) if head else (lane < 64)
        q1, k1, g1 = (jnp.where(own, w, BF(0)) for w in (q, k, g))
        log = jnp.sum(jnp.where(lane == step * 2 + head, logs[...], 0.0), axis=1, keepdims=True)
        probs = jnp.exp(mul(q1, k, MT) + mask[...] - log)
        grad_probs = mul(g1, v, MT)
        inner = jnp.sum(grad_probs * probs, axis=1, keepdims=True)
        grad_scores = (probs * (grad_probs - inner)).astype(BF)
        grad_q = grad_q + mul(grad_scores, k1, MM)
        grad_k = grad_k + mul(grad_scores, q1, TM)
        grad_v = grad_v + mul(probs.astype(BF), g1, TM)
    for c, value in enumerate(
        (turn(grad_q * (1.0 / math.sqrt(HD)), tables, -1.0), turn(grad_k, tables, -1.0), grad_v)
    ):
        low = value.astype(BF)
        at = pl.ds(pl.multiple_of(c * 512 + step * 128, 128), 128)
        grad_proj[:, at] = low
        sums = jnp.sum(low.astype(F32), axis=0, keepdims=True)
        grad_bias[pl.ds(c * 8 + 2 * step, 1)] = sums[:, :HD]
        grad_bias[pl.ds(c * 8 + 2 * step + 1, 1)] = sums[:, HD:]


def feed_kernel(*refs):
    second, grads, w, (hidden, pair, t0, t1, t2, t3, held, sems) = refs[:4], refs[4:8], refs[8], refs[9:]
    cuts = [(i * 256, 256) for i in range(5)] + [(1280, 128)]
    copies = []
    for i, (f, width) in enumerate(cuts):
        for c, at, size in ((0, 2 * f, 2 * width), (1, 2816 + f, width)):
            copy = pltpu.make_async_copy(w.at[:, at : at + size], held.at[:, at : at + size], sems.at[i, c])
            copy.start()
            copies.append(copy)
    for i, (f, width) in enumerate(cuts):
        copies[2 * i].wait()
        copies[2 * i + 1].wait()
        for j in range(2):
            rows = slice(j * 256, (j + 1) * 256)
            lhs = jnp.concatenate([second[2 * j][...], second[2 * j + 1][...]], axis=0)
            both = mul(lhs, held[:, 2 * f : 2 * (f + width)], MM)
            lhs = jnp.concatenate([grads[2 * j][...], grads[2 * j + 1][...]], axis=0)
            back = mul(lhs, held[:, 2816 + f : 2816 + f + width], MM)
            for b in range(width // 128):
                gate, up = both[:, b * 256 : b * 256 + 128], both[:, b * 256 + 128 : b * 256 + 256]
                grad = back[:, b * 128 : (b + 1) * 128]
                sig = jax.nn.sigmoid(gate)
                silu = gate * sig
                at = f + b * 128
                hidden[rows, at : at + 128] = (silu * up).astype(BF)
                pair[rows, 2 * at : 2 * at + 128] = (grad * up * (sig + silu * (1.0 - sig))).astype(BF)
                pair[rows, 2 * at + 128 : 2 * at + 256] = (grad * silu).astype(BF)
    for i in range(4):
        columns = slice(i * 512, (i + 1) * 512)
        store_blocks(mul(pair[...], held[columns, :2816], MT), (t0, t1, t2, t3), columns)


def outer_kernel(a0, a1, a2, a3, b, c0, c1, c2, c3, d, out):
    n, m = b.shape[1], d.shape[1]
    a = jnp.concatenate([a0[...], a1[...], a2[...], a3[...]], axis=0)
    c = jnp.concatenate([c0[...], c1[...], c2[...], c3[...]], axis=0)
    out[:, :n] = mul(a, b[...], TM).astype(BF)
    out[:, n : n + m] = mul(c, d[...], TM).astype(BF)


def outer(a, b, c, d, deps=(), tile=256):
    n, m = b.shape[1], d.shape[1]
    left = [pl.BlockSpec((ROWS, tile), lambda i: (0, i))] * 4
    whole = lambda w: pl.BlockSpec((512, w), lambda i: (0, 0))
    return call(
        outer_kernel,
        (*a, b, *c, d),
        [((2048, n + m), BF)],
        deps,
        grid=(2048 // tile,),
        specs=left + [whole(n)] + left + [whole(m)],
        out_specs=[pl.BlockSpec((tile, n + m), lambda i: (i, 0))],
    )[0]


def half_columns(a, b, c, d, extra):
    n, m = b.shape[1], d.shape[1]
    rows = jnp.concatenate([ref[...] for ref in c], axis=0)
    return ((0, n, mul(a[...], b[...], TM)), (n, m, mul(rows, d[...], TM)), (n + m, extra.shape[1], extra[...].astype(F32)))


def their_half_kernel(place, a, b, c0, c1, c2, c3, d, extra, out):
    for begin, width, value in half_columns(a, b, (c0, c1, c2, c3), d, extra):
        out[:, begin : begin + width] = value.astype(BF)


def pieces_of(width):
    cut = -(-width // 256) * 128
    return ((0, 0, width), (1, 0, width), (2, 0, cut), (2, cut, width), (3, 0, width))


def own_half_kernel(place, a, b, c0, c1, c2, c3, d, extra, theirs, *outs):
    one, two = outs[:5], outs[5:10]
    wide = theirs.shape[1]
    split = one[0].shape[-1]
    step = pl.program_id(0)
    for begin, width, value in half_columns(a, b, (c0, c1, c2, c3), d, extra):
        value = (value + theirs[:, begin : begin + width].astype(F32)).astype(BF)
        for z in range(4):
            at = lax.rem(z - place[2] + 4, 4)
            rows = value[z * 64 : (z + 1) * 64]
            for ref, (k, first, last) in zip(one, pieces_of(split)):
                low, high = max(first, begin), min(last, begin + width)
                if low < high:

                    @pl.when(step == k)
                    def _():
                        ref[at, :, low - first : high - first] = rows[:, low - begin : high - begin]

            for ref, (k, first, last) in zip(two, pieces_of(wide - split)):
                low, high = max(first + split, begin), min(last + split, begin + width)
                if low < high:

                    @pl.when(at == k)
                    def _():
                        ref[0, :, low - split - first : high - split - first] = rows[:, low - begin : high - begin]


def relay_kernel(*refs):
    outs = refs[8:]
    for c in range(2):
        ahead, behind, first, rest = refs[4 * c : 4 * c + 4]
        cut = first.shape[-1]
        outs[2 * c][..., :cut] = (ahead[..., :cut].astype(F32) + first[...].astype(F32)).astype(BF)
        outs[2 * c][..., cut:] = ahead[..., cut:]
        outs[2 * c + 1][..., :cut] = behind[..., :cut]
        outs[2 * c + 1][..., cut:] = (behind[..., cut:].astype(F32) + rest[...].astype(F32)).astype(BF)


def outer_half(place, a, b, c, d, extra, split, deps, theirs=None):
    rows = a.shape[0]
    n, m, e = b.shape[1], d.shape[1], extra.shape[1]
    wide = n + m + e
    pick = lambda i, p: 2 * lax.rem(p[1] + i, 4) + p[0]
    left = pl.BlockSpec((rows, 256), lambda i, p: (0, pick(i, p)))
    quarter = [pl.BlockSpec((ROWS, 256), lambda i, p: (0, pick(i, p)))] * 4
    whole = lambda w: pl.BlockSpec((rows, w), lambda i, p: (0, 0))
    flat = pl.BlockSpec((256, wide), lambda i, p: (i, 0))
    specs = [left, whole(n), *quarter, whole(m), pl.BlockSpec((256, e), lambda i, p: (pick(i, p), 0))]
    if theirs is None:
        kernel, args, outs, shapes = their_half_kernel, [], [flat], [(1024, wide)]
    else:
        kernel, args, specs = own_half_kernel, [theirs], specs + [flat]
        shapes = [(4, 64, last - first) for width in (split, wide - split) for _, first, last in pieces_of(width)]
        outs = [pl.BlockSpec(shape, lambda i, p: (0, 0, 0)) for shape in shapes[:5]]
        outs += [pl.BlockSpec((1,) + shape[1:], lambda i, p: (i, 0, 0)) for shape in shapes[5:]]
    count = 1 + len(specs)
    return pl.pallas_call(
        lambda *refs: kernel(*refs[:count], *refs[count + len(deps) :]),
        name=kernel.__name__,
        grid_spec=pltpu.PrefetchScalarGridSpec(
            num_scalar_prefetch=1,
            grid=(4,),
            in_specs=specs + [pl.BlockSpec(memory_space=pl.ANY)] * len(deps),
            out_specs=outs,
        ),
        out_shape=[jax.ShapeDtypeStruct(shape, BF) for shape in shapes],
        compiler_params=pltpu.CompilerParams(vmem_limit_bytes=60 << 20),
    )(place, a, b, *c, d, extra, *args, *deps)


def term_kernel(a, w, place, *refs):
    value = mul(a[...], w[...], MT)
    if len(refs) > 3:
        *n, norm_two, grad_bias, own, pair, far, tail = refs
        gain = jnp.zeros((1, value.shape[1]), F32)
        for j in range(4):
            gain = gain + jnp.sum(value[j * ROWS : (j + 1) * ROWS] * n[j][...].astype(F32), axis=0, keepdims=True)
        none = jnp.zeros((2, value.shape[1]), F32)
        rows = jnp.concatenate([gain, jnp.sum(value, axis=0, keepdims=True), norm_two[...], none, none], axis=0)
        step = pl.program_id(0)
        lane = lane_of(HD)
        for f in range(8):
            two = [jnp.sum(jnp.where(lane == 2 * (step * 8 + f) + j, grad_bias[...], 0.0), axis=1, keepdims=True) for j in (0, 1)]
            tail[f * 64 : (f + 1) * 64] = jnp.concatenate(
                [
                    jnp.concatenate([rows[:, f * 64 : (f + 1) * 64], jnp.zeros((8, 64), F32)], axis=1),
                    jnp.concatenate(two + [jnp.zeros((24, 126), F32)], axis=1),
                    jnp.zeros((32, 128), F32),
                ],
                axis=0,
            ).astype(BF)
        refs = (own, pair, far)
    blocks = [value[j * ROWS : (j + 1) * ROWS].astype(BF) for j in range(4)]
    refs[0][...] = blocks[0]
    refs[2][:ROWS] = blocks[2]

    @pl.when(place[3] == 0)
    def _():
        refs[1][...] = blocks[3]
        refs[2][ROWS:] = blocks[1]

    @pl.when(place[3] == 1)
    def _():
        refs[1][...] = blocks[1]
        refs[2][ROWS:] = blocks[3]


def row_term(a, w, at, place, n=None, norm_two=None, grad_bias=None, deps=(), tile=512):
    rows, depth = a.shape
    block = lambda height: pl.BlockSpec((height, tile), lambda i: (0, i))
    args = [a, w, place]
    specs = [pl.BlockSpec((rows, depth), lambda i: (0, 0)), pl.BlockSpec((tile, depth), lambda i: (i, at))]
    specs += [pl.BlockSpec(memory_space=pltpu.SMEM)]
    shapes = [((ROWS, 2048), BF)] * 2 + [((2 * ROWS, 2048), BF)]
    outs = [block(ROWS)] * 2 + [block(2 * ROWS)]
    if n is not None:
        args += [*n, norm_two, grad_bias]
        specs += [block(ROWS)] * 4 + [block(2), pl.BlockSpec((24, HD), lambda i: (0, 0))]
        shapes = shapes + [((2048, 128), BF)]
        outs = outs + [pl.BlockSpec((tile, 128), lambda i: (i, 0))]
    return call(term_kernel, args, shapes, deps, grid=(2048 // tile,), specs=specs, out_specs=outs)


def fold_rows(own, pair, far, name, deps=()):
    with jax.named_scope(name):
        return call(fold_kernel, (own, pair, shift(far, 2)), [((ROWS, 2048), F32), ((ROWS, 2048), BF)], deps)


def fold_pair(mine, theirs, name):
    with jax.named_scope(name):
        return mine, lax.ppermute(theirs, "yl", [(0, 1), (1, 0)])


def along(v, axis, k):
    return lax.ppermute(v, axis, [(i, (i + k) % 4) for i in range(4)])


def sum_pieces(one, two, axes, name):
    got = [[], []]
    with jax.named_scope(name):
        for k in (2, 1, 3):
            for c, blocks in enumerate((one, two)):
                got[c].append(along(blocks[k], axes[c], k))
    return got, [one[0], two[0]]


def sum_large(one, two, axes):
    blocks = (one, two)
    with jax.named_scope("large_sum"):
        got = [along(blocks[c][i], axes[c], k) for i, k in ((2, 1), (3, 3)) for c in range(2)]
        sent = call(
            relay_kernel,
            (one[1], one[4], got[0], got[2], two[1], two[4], got[1], got[3]),
            [(v.shape, BF) for v in (one[1], one[4], two[1], two[4])],
        )
        got = [along(sent[2 * c + i], axes[c], k) for i, k in ((0, 1), (1, 3)) for c in range(2)]
        return [blocks[c][0].astype(F32) + got[c].astype(F32) + got[2 + c].astype(F32) for c in range(2)], sent


def normal(v):
    centred = v - jnp.mean(v, axis=-1, keepdims=True)
    r = lax.rsqrt(jnp.mean(centred * centred, axis=-1, keepdims=True) + EPS)
    return centred * r, r


def normal_back(n, r, t):
    return r * (t - jnp.mean(t, axis=-1, keepdims=True) - n * jnp.mean(t * n, axis=-1, keepdims=True))


def across(v):
    return lax.ppermute(v, "core", [(0, 1), (1, 0)])


def body(tokens, seq_lengths, norms, w_qkv, qkv_bias, w_out, w_gate_up, w_down, out_grad):
    me = 2 * lax.axis_index("yh") + lax.axis_index("yl")
    place = jnp.stack([lax.axis_index(name) for name in ("core", "x", "z", "yl")]).astype(jnp.int32)
    small = jnp.concatenate(
        [
            norms,
            qkv_bias.astype(F32).reshape(3, 16),
            jnp.pad(seq_lengths.astype(F32), ((0, 0), (0, 12))),
        ],
        axis=0,
    )
    row_shape = [((ROWS, 2048), BF)]
    w_attn = jnp.concatenate([w_qkv[0], w_qkv[1], w_qkv[2], w_out.T], axis=1)
    (small,) = hold([small], (w_attn,))
    w_attn = swap(w_attn)
    n_own = call(normal_kernel, (tokens,), row_shape)[0]
    pieces = [spread(small, k) for k in range(4)]
    lengths = pieces[0][7, :4].astype(jnp.int32)
    smem = pl.BlockSpec(memory_space=pltpu.SMEM)
    vmem = pl.BlockSpec(memory_space=pltpu.VMEM)
    packed = call(pack_kernel, (me.reshape(1), w_attn, *pieces), [((64, 2176), BF)], (n_own,), specs=[smem] + [vmem] * 5)[0]
    attn_full = lax.all_gather(packed, FSDP, axis=0, tiled=True)

    n_rows = spread_rows(n_own, "n_rows")
    w_ffn = swap(
        jnp.concatenate([w_gate_up.reshape(2, 64, 11, 128).transpose(1, 2, 0, 3).reshape(64, 2816), w_down.T], axis=1)
    )
    inputs = swap(tokens)
    mlp_rows = spread_rows(out_grad, "grad_rows")
    ffn_full = lax.all_gather(w_ffn, FSDP, axis=0, tiled=True)

    extras = attn_full[:, 2048:].reshape(32, 64, 128)
    norm_all = extras[:, :12, :64].astype(F32).reshape(32, 3, 4, 64).sum(axis=1)
    norm_all = norm_all.transpose(1, 0, 2).reshape(4, 2048)
    bias = extras[:, 12, :48].astype(F32).reshape(32, 3, 8, 2).transpose(1, 2, 0, 3).reshape(3, 2, 256)

    places = (((me - jnp.arange(4, dtype=jnp.int32)) % 4) * ROWS)[:, None] + jnp.arange(ROWS, dtype=jnp.int32)
    places = places.reshape(512)
    ends = jnp.cumsum(lengths)
    segment = jnp.sum((places[:, None] >= ends[None, :]).astype(jnp.int32), axis=1)
    begin = jnp.sum(
        jnp.where(jnp.arange(4, dtype=jnp.int32)[None, :] == segment[:, None], (ends - lengths)[None, :], 0), axis=1
    )
    position = places - begin
    rates = jnp.exp(jnp.arange(ROT // 2, dtype=F32) * (-2.0 * math.log(10000.0) / ROT))
    angles = position.astype(F32)[:, None] * rates[None, :]
    cosine, sine = jnp.cos(angles), jnp.sin(angles)
    zero, one = jnp.zeros((512, 8), F32), jnp.ones((512, 48), F32)
    still = jnp.zeros((512, 48), F32)
    tables = (
        jnp.concatenate([cosine, cosine, one] * 2, axis=1),
        jnp.concatenate([-sine, zero, still] * 2, axis=1),
        jnp.concatenate([zero, sine, still] * 2, axis=1),
    )
    marks = (begin[:, None], places[:, None], places[None, :])

    sticky = lambda *shape: pl.BlockSpec(shape, lambda i: (0,) * len(shape))
    part = lambda first: pl.BlockSpec((2048, 256), lambda i: (0, first + i))
    table_specs = [sticky(512, 128)] * 3 + [sticky(512, 1)] * 2 + [sticky(1, 512)]
    first, query, keys, values, logs, mixed, *term = call(
        attend_kernel,
        (*n_rows, norm_all, *[attn_full] * 4, bias, *tables, *marks),
        [((512, 2048), BF)] + [((512, 512), BF)] * 3 + [((512, 128), F32), ((512, 512), BF)] + block_shapes(),
        (w_ffn, inputs),
        grid=(2,),
        specs=[sticky(ROWS, 2048)] * 4
        + [sticky(4, 2048), part(0), part(2), part(4), pl.BlockSpec((2048, 512), lambda i: (0, 3)), sticky(3, 2, 256)]
        + table_specs,
        out_specs=[sticky(512, 2048)]
        + [sticky(512, 512)] * 3
        + [sticky(512, 128), sticky(512, 512)]
        + [sticky(ROWS, 2048)] * 4,
        scratch=[pltpu.VMEM((512, 512), F32)],
    )
    term = hold(term, mlp_rows)
    middle, second = call(middle_kernel, (inputs, norm_all, *scatter_rows(term, "attn_sum")), [((ROWS, 2048), F32)] + row_shape)
    second = gather_rows(second, "second_rows")
    hidden, grad_pair, *term = call(
        feed_kernel,
        (*second, *mlp_rows, ffn_full),
        [((512, 1408), BF), ((512, 2816), BF)] + block_shapes(),
        specs=[pl.BlockSpec(memory_space=pltpu.VMEM)] * 8 + [pl.BlockSpec(memory_space=pl.ANY)],
        scratch=[pltpu.VMEM((2048, 4224), BF), pltpu.SemaphoreType.DMA((6, 2))],
    )
    term = scatter_rows(term, "second_sum")
    grad_ffn = outer(second, grad_pair, mlp_rows, hidden)
    last_term = row_term(hidden, ffn_full, 2, place, deps=(grad_ffn,))
    grad_rows, norm_two = call(
        back_kernel,
        (middle, norm_all, mlp_rows[0], *term),
        row_shape + [((2, 2048), F32)],
        (last_term[0],),
    )
    (grad_ffn,) = hold([grad_ffn], (grad_rows,))
    ffn_low = swap(lax.psum_scatter(grad_ffn, FSDP, scatter_dimension=0, tiled=True))
    ffn_sum = ffn_low.astype(F32)
    attn_rows = gather_rows(grad_rows, "middle_rows")
    last_term = fold_rows(*hold(last_term, attn_rows[1:]), "out_sum")
    column = pl.BlockSpec((512, 128), lambda i: (0, i))
    grad_proj, grad_bias = call(
        attend_back_kernel,
        (*attn_rows, attn_full, query, keys, values, logs, *tables, *marks),
        [((512, 1536), BF), ((24, HD), F32)],
        grid=(4,),
        specs=[sticky(ROWS, 2048)] * 4
        + [pl.BlockSpec((2048, 512), lambda i: (0, 3)), column, column, column, sticky(512, 128)]
        + table_specs,
        out_specs=[sticky(512, 1536), sticky(24, HD)],
        scratch=[pltpu.VMEM((512, 512), F32), pltpu.VMEM((512, 512), BF)],
    )

    *term, tail = row_term(grad_proj, attn_full, 0, place, n_rows, norm_two, grad_bias)
    place_other = place * jnp.array([-1, 1, 1, 1]) + jnp.array([1, 0, 0, 0])
    theirs = across(outer_half(place_other, first, grad_proj, attn_rows, mixed, tail, 1024, last_term[:1])[0])
    parts = outer_half(place, first, grad_proj, attn_rows, mixed, tail, 1024, (), theirs)
    (one, two), sent = sum_large(parts[:5], parts[5:], "xz")
    first_term = fold_rows(*term, "first_sum", (parts[0],))
    first_term = fold_pair(*first_term, "first_sum_too")
    grad_tokens = swap(call(tokens_kernel, (inputs, norm_all, grad_rows, *first_term), row_shape)[0])
    last_term = fold_pair(*hold(last_term, sent[:1]), "out_sum_too")
    layer_out = swap(call(last_kernel, (middle, *last_term), row_shape)[0])
    got, owns = sum_pieces(one.astype(BF), two.astype(BF), "zx", "small_sum")
    owns = hold(owns, (ffn_low, grad_tokens, layer_out))
    one, two = (sum((v.astype(F32) for v in more), own.astype(F32)) for own, more in zip(owns, got))
    one = one.astype(BF)
    small = two[:32, 1024:].astype(F32)
    attn_grads = swap(jnp.concatenate([one, two[:, :1024].astype(BF)], axis=1)).astype(F32)

    norm_parts = small[:4, :64].reshape(4, 4, 16).transpose(1, 0, 2)
    pick = lambda k: lax.dynamic_index_in_dim(norm_parts, (me - k) % 4, 0, keepdims=False)
    with jax.named_scope("norm_sum"):
        got = collect(jnp.concatenate([pick(0), small[8:, :2].reshape(3, 16)], axis=0), 0)
        grad_norms = got[:4] + collect(pick(1), 1) + collect(pick(2), 2) + collect(pick(3), 3)
    return (
        layer_out,
        grad_tokens,
        grad_norms,
        attn_grads[:, :1536].reshape(64, 3, 512).transpose(1, 0, 2),
        got[4:].reshape(3, 8, 2),
        attn_grads[:, 1536:2048].T,
        ffn_sum[:, :2816].reshape(64, 11, 2, 128).transpose(2, 0, 1, 3).reshape(2, 64, 1408),
        ffn_sum[:, 2816:].T,
    )


def solution(mesh):
    ring = Mesh(mesh.devices.reshape(4, 2, 4, 2, 2), ALL)
    fsdp, tp = ("x", "yl", "z"), ("yh", "core")
    return jax.shard_map(
        body,
        mesh=ring,
        in_specs=(
            P(ALL, None),
            P(fsdp, None),
            P(None, ALL),
            P(None, fsdp, tp),
            P(None, tp, fsdp),
            P(tp, fsdp),
            P(None, fsdp, tp),
            P(tp, fsdp),
            P(ALL, None),
        ),
        out_specs=(
            P(ALL, None),
            P(ALL, None),
            P(None, ALL),
            P(None, fsdp, tp),
            P(None, tp, fsdp),
            P(tp, fsdp),
            P(None, fsdp, tp),
            P(tp, fsdp),
        ),
        check_vma=False,
    )
```

```python
import math

import jax
import jax.numpy as jnp
from jax import lax
from jax.experimental import pallas as pl
from jax.experimental.pallas import tpu as pltpu
from jax.sharding import Mesh, PartitionSpec as P

HD = 64
ROT = 16
EPS = 1e-05
ROWS = 128
FSDP = ("x", "core", "z")
ALL = ("x", "yl", "z", "yh", "core")
BF = jnp.bfloat16
F32 = jnp.float32


def swap(v):
    return lax.ppermute(v, ("yl", "core"), [(0, 0), (1, 2), (2, 1), (3, 3)])


def ring_index(y):
    return (y % 2) * 2 + (y // 2) % 2


def shift(v, k):
    return lax.ppermute(v, ("yl", "yh"), [(ring_index(y), ring_index((y + k) % 4)) for y in range(4)])


def spread_pairs(k):
    pairs = []
    for g in range(2):
        for yh in range(2):
            for c in range(2):
                y = (2 * yh + c + k) % 4
                pairs.append((g * 4 + yh * 2 + c, (y % 2) * 4 + (y // 2) * 2 + g))
    return pairs


def spread(v, k):
    return lax.ppermute(v, ("yl", "yh", "core"), spread_pairs(k))


def collect(v, k):
    return lax.ppermute(v, ("yl", "yh", "core"), [(b, a) for a, b in spread_pairs(k)])


def gather_rows(piece, name):
    with jax.named_scope(name):
        return [piece] + [shift(piece, k) for k in (1, 2, 3)]


def spread_rows(piece, name):
    with jax.named_scope(name):
        return [spread(piece, k) for k in range(4)]


def scatter_rows(blocks, name):
    with jax.named_scope(name):
        return [blocks[0]] + [shift(blocks[k], -k) for k in (2, 1, 3)]


def collect_rows(blocks, name):
    with jax.named_scope(name):
        return [collect(blocks[k], k) for k in (2, 1, 3, 0)]


def call(kernel, args, outs, deps=(), limit=None, grid=None, specs=None, out_specs=None, scratch=()):
    n, m = len(args), len(deps)
    limit = limit or (60 if grid or scratch else 16)
    whole = pl.BlockSpec(memory_space=pltpu.VMEM)
    return pl.pallas_call(
        lambda *refs: kernel(*refs[:n], *refs[n + m :]),
        name=kernel.__name__,
        **({} if grid is None else {"grid": grid}),
        in_specs=list(specs or [whole] * n) + [pl.BlockSpec(memory_space=pl.ANY)] * m,
        out_specs=list(out_specs or [whole] * len(outs)),
        out_shape=[jax.ShapeDtypeStruct(s, t) for s, t in outs],
        scratch_shapes=list(scratch),
        compiler_params=pltpu.CompilerParams(vmem_limit_bytes=limit << 20),
    )(*args, *deps)


def hold(arrays, deps):
    n, m = len(arrays), len(deps)
    return pl.pallas_call(
        lambda *refs: None,
        name="hold",
        in_specs=[pl.BlockSpec(memory_space=pl.ANY)] * (n + m),
        out_specs=[pl.BlockSpec(memory_space=pl.ANY)] * n,
        out_shape=[jax.ShapeDtypeStruct(v.shape, v.dtype) for v in arrays],
        input_output_aliases={i: i for i in range(n)},
    )(*arrays, *deps)


MM = (((1,), (0,)), ((), ()))
MT = (((1,), (1,)), ((), ()))
TM = (((0,), (0,)), ((), ()))


def mul(a, b, dims):
    return lax.dot_general(a, b, dims, preferred_element_type=F32)


def total(refs):
    value = refs[0][...].astype(F32)
    for ref in refs[1:]:
        value = value + ref[...].astype(F32)
    return value


def pack_kernel(me, w, p0, p1, p2, p3, out):
    out[:, :2048] = w[...]
    norms = jnp.zeros((4, 64), F32)
    for k, piece in enumerate((p0, p1, p2, p3)):
        place = lax.rem(me[0] - k + 4, 4)
        for q in range(4):
            parts = [jnp.zeros((4, 16 * q), F32)] * (q > 0) + [piece[:4]] + [jnp.zeros((4, 48 - 16 * q), F32)] * (q < 3)
            norms = norms + jnp.where(place == q, jnp.concatenate(parts, axis=1), 0.0)
    high = norms.astype(BF).astype(F32)
    middle = (norms - high).astype(BF).astype(F32)
    biases = jnp.concatenate([p0[4:5], p0[5:6], p0[6:7], jnp.zeros((1, 16), F32)], axis=1)
    rows = [high, middle, norms - high - middle, biases, jnp.zeros((51, 64), F32)]
    rows = jnp.concatenate([jnp.concatenate(rows, axis=0), jnp.zeros((64, 64), F32)], axis=1)
    out[:, 2048:] = rows.astype(BF)


def normal_kernel(tokens, n):
    n[...] = normal(tokens[...].astype(F32))[0].astype(BF)


def middle_kernel(tokens, norms, *refs):
    middle = tokens[...].astype(F32) + total(refs[:4])
    refs[4][...] = middle
    refs[5][...] = (normal(middle)[0] * norms[2:3] + norms[3:4]).astype(BF)


def back_kernel(middle, norms, grad, *refs):
    n, r = normal(middle[...])
    part = total(refs[:4])
    value = grad[...].astype(F32) + normal_back(n, r, part * norms[2:3])
    refs[4][...] = value.astype(BF)
    refs[5][0:1] = jnp.sum(part * n, axis=0, keepdims=True)
    refs[5][1:2] = jnp.sum(part, axis=0, keepdims=True)


def tokens_kernel(tokens, norms, grad, *refs):
    n, r = normal(tokens[...].astype(F32))
    refs[2][...] = (grad[...].astype(F32) + normal_back(n, r, total(refs[:2]) * norms[0:1])).astype(BF)


def last_kernel(middle, *refs):
    refs[2][...] = (middle[...] + total(refs[:2])).astype(BF)


def fold_kernel(own, pair, got, mine, theirs):
    mine[...] = own[...].astype(F32) + got[:ROWS].astype(F32)
    theirs[...] = (pair[...].astype(F32) + got[ROWS:].astype(F32)).astype(BF)


def block_shapes(own=F32):
    return [((ROWS, 2048), own)] + [((ROWS, 2048), BF)] * 3


def store_blocks(value, refs, columns):
    for j in range(4):
        refs[j][:, columns] = value[j * ROWS : (j + 1) * ROWS].astype(refs[j].dtype)


def mask_of(begin, place, row):
    return jnp.where((row[...] >= begin[...]) & (row[...] <= place[...]), 0.0, -1e30).astype(F32)


def lane_of(width):
    return lax.broadcasted_iota(jnp.int32, (1, width), 1)


def turn(v, tables, sign):
    straight, ahead, behind = tables
    return v * straight[...] + sign * (pltpu.roll(v, 120, 1) * ahead[...] + pltpu.roll(v, 8, 1) * behind[...])


def attend_kernel(n0, n1, n2, n3, norms, wq, wk, wv, wo, bias, straight, ahead, behind, begin, place, row, *refs):
    first, query, keys, values, logs, mixed, t0, t1, t2, t3, mask = refs
    step = pl.program_id(0)

    @pl.when(step == 0)
    def _():
        for j, n in enumerate((n0, n1, n2, n3)):
            first[j * ROWS : (j + 1) * ROWS] = (n[...].astype(F32) * norms[0:1] + norms[1:2]).astype(BF)
        mask[...] = mask_of(begin, place, row)
        logs[...] = jnp.zeros_like(logs)

    tables = (straight, ahead, behind)
    q4 = mul(first[...], wq[...], MM) + bias[0, pl.ds(step, 1)]
    k4 = mul(first[...], wk[...], MM) + bias[1, pl.ds(step, 1)]
    v4 = (mul(first[...], wv[...], MM) + bias[2, pl.ds(step, 1)]).astype(BF)
    lane = lane_of(128)
    for pair in range(2):
        at = slice(pair * 128, (pair + 1) * 128)
        columns = pl.ds(pl.multiple_of(step * 256 + pair * 128, 128), 128)
        q = (turn(q4[:, at], tables, 1.0).astype(BF) * BF(1.0 / math.sqrt(HD))).astype(BF)
        k = turn(k4[:, at], tables, 1.0).astype(BF)
        v = v4[:, at]
        query[:, columns] = q
        keys[:, columns] = k
        values[:, columns] = v
        result = None
        for head in range(2):
            own = (lane >= 64) if head else (lane < 64)
            scores = mul(jnp.where(own, q, BF(0)), k, MT) + mask[...]
            top = jnp.max(scores, axis=1, keepdims=True)
            shifted = jnp.exp(scores - top)
            whole = jnp.sum(shifted, axis=1, keepdims=True)
            probs = (shifted * (1.0 / whole)).astype(BF)
            out = mul(probs, v, MM)
            result = out if result is None else jnp.where(own, out, result)
            logs[...] = jnp.where(lane == step * 4 + pair * 2 + head, top + jnp.log(whole), logs[...])
        mixed[:, columns] = result.astype(BF)

    @pl.when(step == 1)
    def _():
        for i in range(4):
            columns = slice(i * 512, (i + 1) * 512)
            store_blocks(mul(mixed[...], wo[columns], MT), (t0, t1, t2, t3), columns)


def attend_back_kernel(g0, g1, g2, g3, wo, query, keys, values, logs, straight, ahead, behind, begin, place, row, *refs):
    grad_proj, grad_bias, mask, grad_mixed = refs
    step = pl.program_id(0)

    @pl.when(step == 0)
    def _():
        for j, g in enumerate((g0, g1, g2, g3)):
            grad_mixed[j * ROWS : (j + 1) * ROWS] = mul(g[...], wo[...], MM).astype(BF)
        mask[...] = mask_of(begin, place, row)

    tables = (straight, ahead, behind)
    lane = lane_of(128)
    columns = pl.ds(pl.multiple_of(step * 128, 128), 128)
    q, k, v, g = query[...], keys[...], values[...], grad_mixed[:, columns]
    grad_q = grad_k = grad_v = 0.0
    for head in range(2):
        own = (lane >= 64) if head else (lane < 64)
        q1, k1, g1 = (jnp.where(own, w, BF(0)) for w in (q, k, g))
        log = jnp.sum(jnp.where(lane == step * 2 + head, logs[...], 0.0), axis=1, keepdims=True)
        probs = jnp.exp(mul(q1, k, MT) + mask[...] - log)
        grad_probs = mul(g1, v, MT)
        inner = jnp.sum(grad_probs * probs, axis=1, keepdims=True)
        grad_scores = (probs * (grad_probs - inner)).astype(BF)
        grad_q = grad_q + mul(grad_scores, k1, MM)
        grad_k = grad_k + mul(grad_scores, q1, TM)
        grad_v = grad_v + mul(probs.astype(BF), g1, TM)
    for c, value in enumerate(
        (turn(grad_q * (1.0 / math.sqrt(HD)), tables, -1.0), turn(grad_k, tables, -1.0), grad_v)
    ):
        low = value.astype(BF)
        at = pl.ds(pl.multiple_of(c * 512 + step * 128, 128), 128)
        grad_proj[:, at] = low
        sums = jnp.sum(low.astype(F32), axis=0, keepdims=True)
        grad_bias[pl.ds(c * 8 + 2 * step, 1)] = sums[:, :HD]
        grad_bias[pl.ds(c * 8 + 2 * step + 1, 1)] = sums[:, HD:]


def feed_kernel(*refs):
    second, grads, w, (hidden, pair, t0, t1, t2, t3, held, sems) = refs[:4], refs[4:8], refs[8], refs[9:]
    cuts = [(i * 256, 256) for i in range(5)] + [(1280, 128)]
    copies = []
    for i, (f, width) in enumerate(cuts):
        for c, at, size in ((0, 2 * f, 2 * width), (1, 2816 + f, width)):
            copy = pltpu.make_async_copy(w.at[:, at : at + size], held.at[:, at : at + size], sems.at[i, c])
            copy.start()
            copies.append(copy)
    for i, (f, width) in enumerate(cuts):
        copies[2 * i].wait()
        copies[2 * i + 1].wait()
        for j in range(2):
            rows = slice(j * 256, (j + 1) * 256)
            lhs = jnp.concatenate([second[2 * j][...], second[2 * j + 1][...]], axis=0)
            both = mul(lhs, held[:, 2 * f : 2 * (f + width)], MM)
            lhs = jnp.concatenate([grads[2 * j][...], grads[2 * j + 1][...]], axis=0)
            back = mul(lhs, held[:, 2816 + f : 2816 + f + width], MM)
            for b in range(width // 128):
                gate, up = both[:, b * 256 : b * 256 + 128], both[:, b * 256 + 128 : b * 256 + 256]
                grad = back[:, b * 128 : (b + 1) * 128]
                sig = jax.nn.sigmoid(gate)
                silu = gate * sig
                at = f + b * 128
                hidden[rows, at : at + 128] = (silu * up).astype(BF)
                pair[rows, 2 * at : 2 * at + 128] = (grad * up * (sig + silu * (1.0 - sig))).astype(BF)
                pair[rows, 2 * at + 128 : 2 * at + 256] = (grad * silu).astype(BF)
    for i in range(4):
        columns = slice(i * 512, (i + 1) * 512)
        store_blocks(mul(pair[...], held[columns, :2816], MT), (t0, t1, t2, t3), columns)


def outer_kernel(a0, a1, a2, a3, b, c0, c1, c2, c3, d, out):
    n, m = b.shape[1], d.shape[1]
    a = jnp.concatenate([a0[...], a1[...], a2[...], a3[...]], axis=0)
    c = jnp.concatenate([c0[...], c1[...], c2[...], c3[...]], axis=0)
    out[:, :n] = mul(a, b[...], TM).astype(BF)
    out[:, n : n + m] = mul(c, d[...], TM).astype(BF)


def outer(a, b, c, d, deps=(), tile=512):
    n, m = b.shape[1], d.shape[1]
    left = [pl.BlockSpec((ROWS, tile), lambda i: (0, i))] * 4
    whole = lambda w: pl.BlockSpec((512, w), lambda i: (0, 0))
    return call(
        outer_kernel,
        (*a, b, *c, d),
        [((2048, n + m), BF)],
        deps,
        grid=(2048 // tile,),
        specs=left + [whole(n)] + left + [whole(m)],
        out_specs=[pl.BlockSpec((tile, n + m), lambda i: (i, 0))],
    )[0]


def half_columns(a, b, c, d, extra):
    n, m = b.shape[1], d.shape[1]
    rows = jnp.concatenate([ref[...] for ref in c], axis=0)
    return ((0, n, mul(a[...], b[...], TM)), (n, m, mul(rows, d[...], TM)), (n + m, extra.shape[1], extra[...].astype(F32)))


def their_half_kernel(place, a, b, c0, c1, c2, c3, d, extra, out):
    for begin, width, value in half_columns(a, b, (c0, c1, c2, c3), d, extra):
        out[:, begin : begin + width] = value.astype(BF)


def pieces_of(width):
    cut = -(-width // 256) * 128
    return ((0, 0, width), (1, 0, width), (2, 0, cut), (2, cut, width), (3, 0, width))


def own_half_kernel(place, a, b, c0, c1, c2, c3, d, extra, theirs, *outs):
    one, two = outs[:5], outs[5:10]
    wide = theirs.shape[1]
    split = one[0].shape[-1]
    step = pl.program_id(0)
    values = [
        (begin, width, (value + theirs[:, begin : begin + width].astype(F32)).astype(BF))
        for begin, width, value in half_columns(a, b, (c0, c1, c2, c3), d, extra)
    ]

    def store(refs, k, at, z, first_column, columns):
        for ref, (block, first, last) in zip(refs, pieces_of(columns)):
            for begin, width, value in values:
                low, high = max(first + first_column, begin), min(last + first_column, begin + width)
                if block == k and low < high:
                    rows = value[z * 64 : (z + 1) * 64, low - begin : high - begin]
                    ref[at, :, low - first_column - first : high - first_column - first] = rows

    for here in range(4):

        @pl.when(place[2] == here)
        def _():
            for z in range(4):
                store(two, (z - here) % 4, 0, z, split, wide - split)
            for k in range(4):

                @pl.when(step == k)
                def _():
                    for z in range(4):
                        store(one, k, (z - here) % 4, z, 0, split)


def relay_kernel(*refs):
    outs = refs[8:]
    for c in range(2):
        ahead, behind, first, rest = refs[4 * c : 4 * c + 4]
        cut = first.shape[-1]
        outs[2 * c][..., :cut] = (ahead[..., :cut].astype(F32) + first[...].astype(F32)).astype(BF)
        outs[2 * c][..., cut:] = ahead[..., cut:]
        outs[2 * c + 1][..., :cut] = behind[..., :cut]
        outs[2 * c + 1][..., cut:] = (behind[..., cut:].astype(F32) + rest[...].astype(F32)).astype(BF)


def outer_half(place, a, b, c, d, extra, split, deps, theirs=None):
    rows = a.shape[0]
    n, m, e = b.shape[1], d.shape[1], extra.shape[1]
    wide = n + m + e
    pick = lambda i, p: 2 * lax.rem(p[1] + i, 4) + p[0]
    left = pl.BlockSpec((rows, 256), lambda i, p: (0, pick(i, p)))
    quarter = [pl.BlockSpec((ROWS, 256), lambda i, p: (0, pick(i, p)))] * 4
    whole = lambda w: pl.BlockSpec((rows, w), lambda i, p: (0, 0))
    flat = pl.BlockSpec((256, wide), lambda i, p: (i, 0))
    specs = [left, whole(n), *quarter, whole(m), pl.BlockSpec((256, e), lambda i, p: (pick(i, p), 0))]
    if theirs is None:
        kernel, args, outs, shapes = their_half_kernel, [], [flat], [(1024, wide)]
    else:
        kernel, args, specs = own_half_kernel, [theirs], specs + [flat]
        shapes = [(4, 64, last - first) for width in (split, wide - split) for _, first, last in pieces_of(width)]
        outs = [pl.BlockSpec(shape, lambda i, p: (0, 0, 0)) for shape in shapes[:5]]
        outs += [pl.BlockSpec((1,) + shape[1:], lambda i, p: (i, 0, 0)) for shape in shapes[5:]]
    count = 1 + len(specs)
    return pl.pallas_call(
        lambda *refs: kernel(*refs[:count], *refs[count + len(deps) :]),
        name=kernel.__name__,
        grid_spec=pltpu.PrefetchScalarGridSpec(
            num_scalar_prefetch=1,
            grid=(4,),
            in_specs=specs + [pl.BlockSpec(memory_space=pl.ANY)] * len(deps),
            out_specs=outs,
        ),
        out_shape=[jax.ShapeDtypeStruct(shape, BF) for shape in shapes],
        compiler_params=pltpu.CompilerParams(vmem_limit_bytes=60 << 20),
    )(place, a, b, *c, d, extra, *args, *deps)


def term_kernel(a, w, place, *refs):
    value = mul(a[...], w[...], MT)
    if len(refs) > 3:
        *n, norm_two, grad_bias, own, pair, far, tail = refs
        gain = jnp.zeros((1, value.shape[1]), F32)
        for j in range(4):
            gain = gain + jnp.sum(value[j * ROWS : (j + 1) * ROWS] * n[j][...].astype(F32), axis=0, keepdims=True)
        none = jnp.zeros((2, value.shape[1]), F32)
        rows = jnp.concatenate([gain, jnp.sum(value, axis=0, keepdims=True), norm_two[...], none, none], axis=0)
        step = pl.program_id(0)
        lane = lane_of(HD)
        for f in range(8):
            two = [jnp.sum(jnp.where(lane == 2 * (step * 8 + f) + j, grad_bias[...], 0.0), axis=1, keepdims=True) for j in (0, 1)]
            tail[f * 64 : (f + 1) * 64] = jnp.concatenate(
                [
                    jnp.concatenate([rows[:, f * 64 : (f + 1) * 64], jnp.zeros((8, 64), F32)], axis=1),
                    jnp.concatenate(two + [jnp.zeros((24, 126), F32)], axis=1),
                    jnp.zeros((32, 128), F32),
                ],
                axis=0,
            ).astype(BF)
        refs = (own, pair, far)
    blocks = [value[j * ROWS : (j + 1) * ROWS].astype(BF) for j in range(4)]
    refs[0][...] = blocks[0]
    refs[2][:ROWS] = blocks[2]

    @pl.when(place[3] == 0)
    def _():
        refs[1][...] = blocks[3]
        refs[2][ROWS:] = blocks[1]

    @pl.when(place[3] == 1)
    def _():
        refs[1][...] = blocks[1]
        refs[2][ROWS:] = blocks[3]


def row_term(a, w, at, place, n=None, norm_two=None, grad_bias=None, deps=(), tile=512):
    rows, depth = a.shape
    block = lambda height: pl.BlockSpec((height, tile), lambda i: (0, i))
    args = [a, w, place]
    specs = [pl.BlockSpec((rows, depth), lambda i: (0, 0)), pl.BlockSpec((tile, depth), lambda i: (i, at))]
    specs += [pl.BlockSpec(memory_space=pltpu.SMEM)]
    shapes = [((ROWS, 2048), BF)] * 2 + [((2 * ROWS, 2048), BF)]
    outs = [block(ROWS)] * 2 + [block(2 * ROWS)]
    if n is not None:
        args += [*n, norm_two, grad_bias]
        specs += [block(ROWS)] * 4 + [block(2), pl.BlockSpec((24, HD), lambda i: (0, 0))]
        shapes = shapes + [((2048, 128), BF)]
        outs = outs + [pl.BlockSpec((tile, 128), lambda i: (i, 0))]
    return call(term_kernel, args, shapes, deps, grid=(2048 // tile,), specs=specs, out_specs=outs)


def fold_rows(own, pair, far, name, deps=()):
    with jax.named_scope(name):
        return call(fold_kernel, (own, pair, shift(far, 2)), [((ROWS, 2048), F32), ((ROWS, 2048), BF)], deps)


def fold_pair(mine, theirs, name):
    with jax.named_scope(name):
        return mine, lax.ppermute(theirs, "yl", [(0, 1), (1, 0)])


def along(v, axis, k):
    return lax.ppermute(v, axis, [(i, (i + k) % 4) for i in range(4)])


def sum_pieces(one, two, axes, name):
    got = [[], []]
    with jax.named_scope(name):
        for k in (2, 1, 3):
            for c, blocks in enumerate((one, two)):
                got[c].append(along(blocks[k], axes[c], k))
    return got, [one[0], two[0]]


def sum_large(one, two, axes):
    blocks = (one, two)
    with jax.named_scope("large_sum"):
        got = [along(blocks[c][i], axes[c], k) for i, k in ((2, 1), (3, 3)) for c in range(2)]
        sent = call(
            relay_kernel,
            (one[1], one[4], got[0], got[2], two[1], two[4], got[1], got[3]),
            [(v.shape, BF) for v in (one[1], one[4], two[1], two[4])],
        )
        got = [along(sent[2 * c + i], axes[c], k) for i, k in ((0, 1), (1, 3)) for c in range(2)]
        return [blocks[c][0].astype(F32) + got[c].astype(F32) + got[2 + c].astype(F32) for c in range(2)], sent


def normal(v):
    centred = v - jnp.mean(v, axis=-1, keepdims=True)
    r = lax.rsqrt(jnp.mean(centred * centred, axis=-1, keepdims=True) + EPS)
    return centred * r, r


def normal_back(n, r, t):
    return r * (t - jnp.mean(t, axis=-1, keepdims=True) - n * jnp.mean(t * n, axis=-1, keepdims=True))


def across(v):
    return lax.ppermute(v, "core", [(0, 1), (1, 0)])


def body(tokens, seq_lengths, norms, w_qkv, qkv_bias, w_out, w_gate_up, w_down, out_grad):
    me = 2 * lax.axis_index("yh") + lax.axis_index("yl")
    place = jnp.stack([lax.axis_index(name) for name in ("core", "x", "z", "yl")]).astype(jnp.int32)
    small = jnp.concatenate(
        [
            norms,
            qkv_bias.astype(F32).reshape(3, 16),
            jnp.pad(seq_lengths.astype(F32), ((0, 0), (0, 12))),
        ],
        axis=0,
    )
    row_shape = [((ROWS, 2048), BF)]
    w_attn = jnp.concatenate([w_qkv[0], w_qkv[1], w_qkv[2], w_out.T], axis=1)
    (small,) = hold([small], (w_attn,))
    w_attn = swap(w_attn)
    n_own = call(normal_kernel, (tokens,), row_shape)[0]
    pieces = [spread(small, k) for k in range(4)]
    lengths = pieces[0][7, :4].astype(jnp.int32)
    smem = pl.BlockSpec(memory_space=pltpu.SMEM)
    vmem = pl.BlockSpec(memory_space=pltpu.VMEM)
    packed = call(pack_kernel, (me.reshape(1), w_attn, *pieces), [((64, 2176), BF)], (n_own,), specs=[smem] + [vmem] * 5)[0]
    attn_full = lax.all_gather(packed, FSDP, axis=0, tiled=True)

    n_rows = spread_rows(n_own, "n_rows")
    w_ffn = swap(
        jnp.concatenate([w_gate_up.reshape(2, 64, 11, 128).transpose(1, 2, 0, 3).reshape(64, 2816), w_down.T], axis=1)
    )
    inputs = swap(tokens)
    mlp_rows = spread_rows(out_grad, "grad_rows")
    ffn_full = lax.all_gather(w_ffn, FSDP, axis=0, tiled=True)

    extras = attn_full[:, 2048:].reshape(32, 64, 128)
    norm_all = extras[:, :12, :64].astype(F32).reshape(32, 3, 4, 64).sum(axis=1)
    norm_all = norm_all.transpose(1, 0, 2).reshape(4, 2048)
    bias = extras[:, 12, :48].astype(F32).reshape(32, 3, 8, 2).transpose(1, 2, 0, 3).reshape(3, 2, 256)

    places = (((me - jnp.arange(4, dtype=jnp.int32)) % 4) * ROWS)[:, None] + jnp.arange(ROWS, dtype=jnp.int32)
    places = places.reshape(512)
    ends = jnp.cumsum(lengths)
    segment = jnp.sum((places[:, None] >= ends[None, :]).astype(jnp.int32), axis=1)
    begin = jnp.sum(
        jnp.where(jnp.arange(4, dtype=jnp.int32)[None, :] == segment[:, None], (ends - lengths)[None, :], 0), axis=1
    )
    position = places - begin
    rates = jnp.exp(jnp.arange(ROT // 2, dtype=F32) * (-2.0 * math.log(10000.0) / ROT))
    angles = position.astype(F32)[:, None] * rates[None, :]
    cosine, sine = jnp.cos(angles), jnp.sin(angles)
    zero, one = jnp.zeros((512, 8), F32), jnp.ones((512, 48), F32)
    still = jnp.zeros((512, 48), F32)
    tables = (
        jnp.concatenate([cosine, cosine, one] * 2, axis=1),
        jnp.concatenate([-sine, zero, still] * 2, axis=1),
        jnp.concatenate([zero, sine, still] * 2, axis=1),
    )
    marks = (begin[:, None], places[:, None], places[None, :])

    sticky = lambda *shape: pl.BlockSpec(shape, lambda i: (0,) * len(shape))
    part = lambda first: pl.BlockSpec((2048, 256), lambda i: (0, first + i))
    table_specs = [sticky(512, 128)] * 3 + [sticky(512, 1)] * 2 + [sticky(1, 512)]
    first, query, keys, values, logs, mixed, *term = call(
        attend_kernel,
        (*n_rows, norm_all, *[attn_full] * 4, bias, *tables, *marks),
        [((512, 2048), BF)] + [((512, 512), BF)] * 3 + [((512, 128), F32), ((512, 512), BF)] + block_shapes(),
        (w_ffn, inputs),
        grid=(2,),
        specs=[sticky(ROWS, 2048)] * 4
        + [sticky(4, 2048), part(0), part(2), part(4), pl.BlockSpec((2048, 512), lambda i: (0, 3)), sticky(3, 2, 256)]
        + table_specs,
        out_specs=[sticky(512, 2048)]
        + [sticky(512, 512)] * 3
        + [sticky(512, 128), sticky(512, 512)]
        + [sticky(ROWS, 2048)] * 4,
        scratch=[pltpu.VMEM((512, 512), F32)],
    )
    term = hold(term, mlp_rows)
    middle, second = call(middle_kernel, (inputs, norm_all, *scatter_rows(term, "attn_sum")), [((ROWS, 2048), F32)] + row_shape)
    second = gather_rows(second, "second_rows")
    hidden, grad_pair, *term = call(
        feed_kernel,
        (*second, *mlp_rows, ffn_full),
        [((512, 1408), BF), ((512, 2816), BF)] + block_shapes(),
        specs=[pl.BlockSpec(memory_space=pltpu.VMEM)] * 8 + [pl.BlockSpec(memory_space=pl.ANY)],
        scratch=[pltpu.VMEM((2048, 4224), BF), pltpu.SemaphoreType.DMA((6, 2))],
    )
    term = scatter_rows(term, "second_sum")
    grad_ffn = outer(second, grad_pair, mlp_rows, hidden)
    last_term = row_term(hidden, ffn_full, 2, place, deps=(grad_ffn,))
    grad_rows, norm_two = call(
        back_kernel,
        (middle, norm_all, mlp_rows[0], *term),
        row_shape + [((2, 2048), F32)],
        (last_term[0],),
    )
    (grad_ffn,) = hold([grad_ffn], (grad_rows,))
    ffn_low = swap(lax.psum_scatter(grad_ffn, FSDP, scatter_dimension=0, tiled=True))
    ffn_sum = ffn_low.astype(F32)
    attn_rows = gather_rows(grad_rows, "middle_rows")
    last_term = fold_rows(*hold(last_term, attn_rows[1:]), "out_sum")
    column = pl.BlockSpec((512, 128), lambda i: (0, i))
    grad_proj, grad_bias = call(
        attend_back_kernel,
        (*attn_rows, attn_full, query, keys, values, logs, *tables, *marks),
        [((512, 1536), BF), ((24, HD), F32)],
        grid=(4,),
        specs=[sticky(ROWS, 2048)] * 4
        + [pl.BlockSpec((2048, 512), lambda i: (0, 3)), column, column, column, sticky(512, 128)]
        + table_specs,
        out_specs=[sticky(512, 1536), sticky(24, HD)],
        scratch=[pltpu.VMEM((512, 512), F32), pltpu.VMEM((512, 512), BF)],
    )

    *term, tail = row_term(grad_proj, attn_full, 0, place, n_rows, norm_two, grad_bias)
    place_other = place * jnp.array([-1, 1, 1, 1]) + jnp.array([1, 0, 0, 0])
    theirs = across(outer_half(place_other, first, grad_proj, attn_rows, mixed, tail, 1024, last_term[:1])[0])
    parts = outer_half(place, first, grad_proj, attn_rows, mixed, tail, 1024, (), theirs)
    (one, two), sent = sum_large(parts[:5], parts[5:], "xz")
    first_term = fold_rows(*term, "first_sum", (parts[0],))
    first_term = fold_pair(*first_term, "first_sum_too")
    grad_tokens = swap(call(tokens_kernel, (inputs, norm_all, grad_rows, *first_term), row_shape)[0])
    last_term = fold_pair(*hold(last_term, sent[:1]), "out_sum_too")
    layer_out = swap(call(last_kernel, (middle, *last_term), row_shape)[0])
    got, owns = sum_pieces(one.astype(BF), two.astype(BF), "zx", "small_sum")
    owns = hold(owns, (ffn_low, grad_tokens, layer_out))
    one, two = (sum((v.astype(F32) for v in more), own.astype(F32)) for own, more in zip(owns, got))
    one = one.astype(BF)
    small = two[:32, 1024:].astype(F32)
    attn_grads = swap(jnp.concatenate([one, two[:, :1024].astype(BF)], axis=1)).astype(F32)

    norm_parts = small[:4, :64].reshape(4, 4, 16).transpose(1, 0, 2)
    pick = lambda k: lax.dynamic_index_in_dim(norm_parts, (me - k) % 4, 0, keepdims=False)
    with jax.named_scope("norm_sum"):
        got = collect(jnp.concatenate([pick(0), small[8:, :2].reshape(3, 16)], axis=0), 0)
        grad_norms = got[:4] + collect(pick(1), 1) + collect(pick(2), 2) + collect(pick(3), 3)
    return (
        layer_out,
        grad_tokens,
        grad_norms,
        attn_grads[:, :1536].reshape(64, 3, 512).transpose(1, 0, 2),
        got[4:].reshape(3, 8, 2),
        attn_grads[:, 1536:2048].T,
        ffn_sum[:, :2816].reshape(64, 11, 2, 128).transpose(2, 0, 1, 3).reshape(2, 64, 1408),
        ffn_sum[:, 2816:].T,
    )


def solution(mesh):
    ring = Mesh(mesh.devices.reshape(4, 2, 4, 2, 2), ALL)
    fsdp, tp = ("x", "yl", "z"), ("yh", "core")
    return jax.shard_map(
        body,
        mesh=ring,
        in_specs=(
            P(ALL, None),
            P(fsdp, None),
            P(None, ALL),
            P(None, fsdp, tp),
            P(None, tp, fsdp),
            P(tp, fsdp),
            P(None, fsdp, tp),
            P(tp, fsdp),
            P(ALL, None),
        ),
        out_specs=(
            P(ALL, None),
            P(ALL, None),
            P(None, ALL),
            P(None, fsdp, tp),
            P(None, tp, fsdp),
            P(tp, fsdp),
            P(None, fsdp, tp),
            P(tp, fsdp),
        ),
        check_vma=False,
    )
```
